32 devices in a mesh: ctx: 4 (over y, core), exp: 8 (over z, x).
Axes of the slice: x: 2, y: 2, z: 4, core: 2. Of those that a mesh axis runs over, the one named last changes fastest.
Arguments:
- queries: bfloat16 [1024, 8192], P('exp', 'ctx'), may hold values from -180 to 180
- key_proj: bfloat16 [1024, 512], P('exp'), may hold values from -7 to 7
- value_matrix_rows: bfloat16 [1024, 512], P('exp'), may hold values from -6 to 6
- attn_grad: bfloat16 [1024, 8192], P('exp', 'ctx'), may hold values from -6 to 6
- moe_input: bfloat16 [1024, 4096], P('exp', 'ctx'), may hold values from -6 to 6
- moe_grad: bfloat16 [1024, 4096], P('exp', 'ctx'), may hold values from -6 to 6
- expert_ids: int32 [1024, 2], P('exp'), may hold values from 0 to 15, as said below
- route_weights: float32 [1024, 2], P('exp'), may hold values from 0.1 to 1
- gate_proj: bfloat16 [16, 4096, 768], P('exp', 'ctx'), may hold values from -0.09375 to 0.09375
- up_proj: bfloat16 [16, 4096, 768], P('exp', 'ctx'), may hold values from -0.09375 to 0.09375
- down_proj: bfloat16 [16, 768, 4096], P('exp', None, 'ctx'), may hold values from -0.21875 to 0.21875
Outputs:
- attn_out: bfloat16 [1024, 8192], P('exp', 'ctx')
- query_grad: bfloat16 [1024, 8192], P('exp', 'ctx')
- key_grad: bfloat16 [1024, 512], P('exp')
- value_grad: bfloat16 [1024, 512], P('exp')
- moe_out: bfloat16 [1024, 4096], P('exp', 'ctx')
- input_grad: bfloat16 [1024, 4096], P('exp', 'ctx')
The draws below stay inside these ranges and needn't reach their ends.
Inputs may be any that keep to these rules, and one draw needn't show every extreme that they name: `expert_ids`: each row names 2 different experts. In each aligned block of 128 rows no expert is named more than 18 times, and one expert, the same in every block, is named exactly 18 times in every block.
All inputs are finite; a program needn't handle non-finite values.
Results may differ from the reference program's by a relative error of at most 0.019.
Values may be sent and summed in bfloat16 or wider, within the bound.
No kernel may reach another device: no remote copies, remote signals or barrier semaphores. Data moves between devices by JAX's collectives and lax.ppermute only.
A program may use at most 64 MiB of HBM per device.

```python
import jax
import jax.numpy as jnp
from jax import lax

D = 4096
QUERY_HEAD_COUNT = 64
KEY_VALUE_HEADS = 4
HEAD_SIZE = 128
FF = 768
TOP = 2
TOK_DEV = 128
SEQUENCE_TOKENS = 1024
EXPERTS = 16
SLOT = 18
CAP = 144


def drawn_pair(key):
    query = jnp.clip(jax.random.normal(jax.random.fold_in(key, 101), (SEQUENCE_TOKENS, QUERY_HEAD_COUNT * HEAD_SIZE), jnp.float32), -6.0, 6.0)
    key_row_block = jnp.clip(jax.random.normal(jax.random.fold_in(key, 102), (SEQUENCE_TOKENS, KEY_VALUE_HEADS * HEAD_SIZE), jnp.float32), -6.0, 6.0)
    return (query, key_row_block)


def draw_queries(key, part):
    return drawn_pair(key)[0].astype(jnp.bfloat16)


def draw_key_proj(key, part):
    return drawn_pair(key)[1].astype(jnp.bfloat16)


def draw_expert_ids(key, part):
    others = EXPERTS - 1
    busiest = jax.random.randint(jax.random.fold_in(key, 201), (), 0, EXPERTS).astype(jnp.int32)
    block_count = SEQUENCE_TOKENS // TOK_DEV

    def one_block(block_index):
        block_key = jax.random.fold_in(jax.random.fold_in(key, 301), block_index)
        ranking = jax.random.permutation(jax.random.fold_in(block_key, 1), others).astype(jnp.int32)
        ranking = ranking + (ranking >= busiest).astype(jnp.int32)
        spots = jnp.arange(2 * TOK_DEV, dtype=jnp.int32)
        rest = jnp.maximum(spots - SLOT, 0) // SLOT
        rest = jnp.minimum(rest, others - 1)
        labels = jnp.where(spots < SLOT, busiest, ranking[rest]).astype(jnp.int32)
        first = labels[:TOK_DEV]
        second = labels[TOK_DEV:]
        flip = jax.random.randint(jax.random.fold_in(block_key, 3), (TOK_DEV,), 0, 2).astype(jnp.int32)
        left = jnp.where(flip == 1, second, first)
        right = jnp.where(flip == 1, first, second)
        order = jax.random.permutation(jax.random.fold_in(block_key, 2), TOK_DEV).astype(jnp.int32)
        return jnp.stack([left[order], right[order]], axis=1)
    table = jax.vmap(one_block)(jnp.arange(block_count, dtype=jnp.int32))
    return table.reshape(SEQUENCE_TOKENS, 2).astype(jnp.int32)


def steps_of(stream_key, shape, split, low, top_value):
    level = 1.0
    for dim, blocks in split:
        steps = jax.random.uniform(jax.random.fold_in(jax.random.fold_in(stream_key, 6), dim), (blocks,), jnp.float32, low / len(split), top_value / len(split))
        level = level * jnp.repeat(jnp.exp(steps), shape[dim] // blocks).reshape((-1,) + (1,) * (len(shape) - 1 - dim))
    return level


def normal_values(key, dims, width, reach, split=(), kind=jnp.bfloat16):
    gain = steps_of(key, dims, split, -0.22, 0.18) if split else 1.0
    values = jax.random.normal(key, dims, jnp.float32) * width * gain
    return jnp.minimum(jnp.maximum(values, -reach), reach).astype(kind)


def setup_inputs(seed: int = 0) -> dict:
    key_of = jax.random.split(jax.random.key(seed), 12)
    queries = draw_queries(jax.random.fold_in(key_of[11], 71), 0)
    key_proj = draw_key_proj(jax.random.fold_in(key_of[11], 71), 0)
    value_matrix_rows = normal_values(key_of[2], (SEQUENCE_TOKENS, KEY_VALUE_HEADS * HEAD_SIZE), 1.0, 6.0, ((0, 8),))
    attn_grad = normal_values(key_of[3], (SEQUENCE_TOKENS, QUERY_HEAD_COUNT * HEAD_SIZE), 1.0, 6.0, ((0, 8), (1, 4)))
    moe_input = normal_values(key_of[4], (SEQUENCE_TOKENS, D), 1.0, 6.0, ((0, 8), (1, 4)))
    moe_grad = normal_values(key_of[5], (SEQUENCE_TOKENS, D), 1.0, 6.0, ((0, 8), (1, 4)))
    expert_ids = draw_expert_ids(jax.random.fold_in(key_of[11], 71), 0)
    route_weights = jnp.clip(0.1 + 0.9 * jax.random.uniform(key_of[7], (SEQUENCE_TOKENS, TOP), jnp.float32) ** steps_of(key_of[7], (SEQUENCE_TOKENS, TOP), ((0, 8),), -0.2, 0.2), 0.1, 1.0)
    gate_proj = normal_values(key_of[8], (EXPERTS, D, FF), D ** -0.5, 0.09375, ((0, 8), (1, 4)))
    up_proj = normal_values(key_of[9], (EXPERTS, D, FF), D ** -0.5, 0.09375, ((0, 8), (1, 4)))
    down_proj = normal_values(key_of[10], (EXPERTS, FF, D), FF ** -0.5, 0.21875, ((0, 8), (2, 4)))
    return dict(queries=queries, key_proj=key_proj, value_matrix_rows=value_matrix_rows, attn_grad=attn_grad, moe_input=moe_input, moe_grad=moe_grad, expert_ids=expert_ids, route_weights=route_weights, gate_proj=gate_proj, up_proj=up_proj, down_proj=down_proj)


def head_pass(query_head, cotan_head, key_head, value_head, positions):
    score_scale = HEAD_SIZE ** -0.5
    scores = jnp.dot(query_head, key_head.T, preferred_element_type=jnp.float32) * score_scale
    scores = jnp.where(positions[None, :] <= positions[:, None], scores, -jnp.inf)
    log_total = jax.nn.logsumexp(scores, axis=1, keepdims=True)
    attn_probs = jnp.exp(scores - log_total).astype(jnp.bfloat16)
    attended = jnp.dot(attn_probs, value_head, preferred_element_type=jnp.float32).astype(jnp.bfloat16)
    row_dot = jnp.sum(cotan_head.astype(jnp.float32) * attended.astype(jnp.float32), axis=1, keepdims=True)
    prob_grad = jnp.dot(cotan_head, value_head.T, preferred_element_type=jnp.float32)
    score_grad = (attn_probs.astype(jnp.float32) * (prob_grad - row_dot)).astype(jnp.bfloat16)
    query_back = (jnp.dot(score_grad, key_head, preferred_element_type=jnp.float32) * score_scale).astype(jnp.bfloat16)
    key_term = jnp.dot(score_grad.T, query_head, preferred_element_type=jnp.float32)
    value_term = jnp.dot(attn_probs.T, cotan_head, preferred_element_type=jnp.float32)
    return attended, query_back, key_term, value_term


def reference(queries, key_proj, value_matrix_rows, attn_grad, moe_input, moe_grad, expert_ids, route_weights, gate_proj, up_proj, down_proj):
    positions = jnp.arange(SEQUENCE_TOKENS, dtype=jnp.int32)
    query_group_width = QUERY_HEAD_COUNT // KEY_VALUE_HEADS
    query_heads = queries.reshape(SEQUENCE_TOKENS, QUERY_HEAD_COUNT, HEAD_SIZE).transpose(1, 0, 2)
    cotan_heads = attn_grad.reshape(SEQUENCE_TOKENS, QUERY_HEAD_COUNT, HEAD_SIZE).transpose(1, 0, 2)
    out_list = []
    qgrad_list = []
    kgrad_list = []
    vgrad_list = []
    for key_value_index in range(KEY_VALUE_HEADS):
        key_head = key_proj[:, key_value_index * HEAD_SIZE:(key_value_index + 1) * HEAD_SIZE]
        value_head = value_matrix_rows[:, key_value_index * HEAD_SIZE:(key_value_index + 1) * HEAD_SIZE]

        def one_head(pair, key_head=key_head, value_head=value_head):
            return head_pass(pair[0], pair[1], key_head, value_head, positions)

        attended, query_back, key_term, value_term = lax.map(
            one_head,
            (query_heads[key_value_index * query_group_width:(key_value_index + 1) * query_group_width],
             cotan_heads[key_value_index * query_group_width:(key_value_index + 1) * query_group_width]))
        out_list.append(attended)
        qgrad_list.append(query_back)
        kgrad_list.append((jnp.sum(key_term, axis=0) * (HEAD_SIZE ** -0.5)).astype(jnp.bfloat16))
        vgrad_list.append(jnp.sum(value_term, axis=0).astype(jnp.bfloat16))
    attn_out = jnp.concatenate(out_list, axis=0).transpose(1, 0, 2).reshape(SEQUENCE_TOKENS, QUERY_HEAD_COUNT * HEAD_SIZE)
    query_grad = jnp.concatenate(qgrad_list, axis=0).transpose(1, 0, 2).reshape(SEQUENCE_TOKENS, QUERY_HEAD_COUNT * HEAD_SIZE)
    key_grad = jnp.concatenate(kgrad_list, axis=1)
    value_grad = jnp.concatenate(vgrad_list, axis=1)

    flat_ids = expert_ids.reshape(-1)
    flat_gain = route_weights.reshape(-1)

    def expert_step(carry, inputs):
        out_acc, grad_acc = carry
        expert_index, gate_w, up_w, down_w = inputs
        chosen = flat_ids == expert_index
        places = jnp.nonzero(chosen, size=CAP, fill_value=0)[0]
        filled = jnp.arange(CAP) < jnp.sum(chosen)
        token_of = (places // TOP).astype(jnp.int32)
        picked_gain = flat_gain[places]
        route_gain = jnp.where(filled, picked_gain, jnp.zeros_like(picked_gain))
        rows_in = moe_input[token_of]
        gate = jnp.dot(rows_in, gate_w, preferred_element_type=jnp.float32)
        up_term = jnp.dot(rows_in, up_w, preferred_element_type=jnp.float32)
        sigmoid_gate = jax.nn.sigmoid(gate)
        activated = gate * sigmoid_gate
        hidden = (activated * up_term).astype(jnp.bfloat16)
        route_out = jnp.dot(hidden, down_w, preferred_element_type=jnp.float32).astype(jnp.bfloat16)
        scaled = (moe_grad[token_of].astype(jnp.float32) * route_gain[:, None]).astype(jnp.bfloat16)
        hidden_grad = jnp.dot(scaled, down_w.T, preferred_element_type=jnp.float32)
        gate_back = (hidden_grad * up_term * sigmoid_gate * (1.0 + gate * (1.0 - sigmoid_gate))).astype(jnp.bfloat16)
        up_back = (hidden_grad * activated).astype(jnp.bfloat16)
        route_in = (jnp.dot(gate_back, gate_w.T, preferred_element_type=jnp.float32)
                    + jnp.dot(up_back, up_w.T, preferred_element_type=jnp.float32)).astype(jnp.bfloat16)
        out_terms = route_out.astype(jnp.float32) * route_gain[:, None]
        in_terms = jnp.where(filled[:, None], route_in.astype(jnp.float32), jnp.zeros_like(route_in, dtype=jnp.float32))
        out_acc = out_acc + jax.ops.segment_sum(out_terms, token_of, num_segments=SEQUENCE_TOKENS)
        grad_acc = grad_acc + jax.ops.segment_sum(in_terms, token_of, num_segments=SEQUENCE_TOKENS)
        return (out_acc, grad_acc), None

    start = (jnp.zeros((SEQUENCE_TOKENS, D), jnp.float32), jnp.zeros((SEQUENCE_TOKENS, D), jnp.float32))
    (out_acc, grad_acc), unused = lax.scan(
        expert_step, start, (jnp.arange(EXPERTS, dtype=jnp.int32), gate_proj, up_proj, down_proj))
    moe_out = out_acc.astype(jnp.bfloat16)
    input_grad = grad_acc.astype(jnp.bfloat16)
    return (attn_out, query_grad, key_grad, value_grad, moe_out, input_grad)
```

```python
import functools
import math

import jax
import jax.numpy as jnp
from jax import lax
from jax.experimental import pallas as pl
from jax.experimental.pallas import tpu as pltpu
from jax.sharding import PartitionSpec as P

HEAD_SIZE = 128
LANES = 128
ROW_TILE = 16
VMEM_BYTES = 48 * 1024 * 1024
BF16 = jnp.bfloat16
F32 = jnp.float32


def dot(a, b, a_dim=1, b_dim=0):
    return lax.dot_general(a, b, (((a_dim,), (b_dim,)), ((), ())), preferred_element_type=F32)


def iota(shape, dim):
    return lax.broadcasted_iota(jnp.int32, shape, dim)


def params(steps=1):
    return pltpu.CompilerParams(
        vmem_limit_bytes=VMEM_BYTES, dimension_semantics=("arbitrary",) * steps
    )


def cost(flops, bytes_accessed, transcendentals=0):
    return pl.CostEstimate(
        flops=int(flops), bytes_accessed=int(bytes_accessed), transcendentals=int(transcendentals)
    )


def power_of_two(value):
    return value > 0 and value & (value - 1) == 0


class Slots:
    def __init__(self, slot_count, width, exp_count, local_experts):
        whole = slot_count // ROW_TILE * ROW_TILE
        rem = slot_count - whole
        blocks = width // LANES
        self.fold = (
            whole > 0
            and rem > 0
            and power_of_two(rem)
            and power_of_two(exp_count)
            and rem * blocks <= whole
            and (rem * exp_count) % ROW_TILE == 0
        )
        self.rows = whole if self.fold or rem == 0 else whole + ROW_TILE
        self.rem = rem if self.fold else 0
        self.blocks = blocks
        self.width = width
        self.columns = width + (LANES if self.fold else 0)
        self.exp_count = exp_count
        self.local = local_experts
        self.experts = exp_count * local_experts
        self.total = self.experts * self.rows
        self.per_expert = exp_count * (self.rows + self.rem)


def route_places(ids, slots):
    tokens, top = ids.shape
    lanes = -(-slots.experts // LANES) * LANES
    expert = iota((tokens, lanes), 1)
    hits = [(ids[:, r : r + 1] == expert).astype(F32) for r in range(top)]
    earlier = (iota((tokens, tokens), 0) > iota((tokens, tokens), 1)).astype(BF16)
    before = dot(earlier, sum(hits).astype(BF16))
    found = []
    for r in range(top):
        rank = jnp.sum(hits[r] * before, axis=1, keepdims=True)
        base = ids[:, r : r + 1].astype(F32) * slots.rows
        inside = rank < slots.rows
        main = jnp.where(inside, base + rank, -1.0)
        folded = jnp.where(inside, -65536.0, base + rank - slots.rows)
        found.append((main, folded))
    return found


def as_row(column):
    tokens = column.shape[0]
    return jnp.transpose(jnp.broadcast_to(column, (tokens, LANES)))[0:1, :]


def dispatch_kernel(slots, weighted, ids_ref, gain_ref, rows_ref, out_ref):
    tokens, top = ids_ref.shape
    places = route_places(ids_ref[...], slots)
    mains = [as_row(main) for main, _ in places]
    folds = [as_row(folded) for _, folded in places]
    gains = [as_row(gain_ref[:, r : r + 1]) for r in range(top)]
    slot = iota((slots.total, tokens), 0).astype(F32)
    rows = rows_ref[...]

    def picks(wanted):
        pick = jnp.zeros((slots.total, tokens), F32)
        gain = pick
        for r in range(top):
            here = slot == wanted[r]
            pick = jnp.where(here, 1.0, pick)
            gain = jnp.where(here, gains[r], gain)
        return pick.astype(BF16), gain

    pick, gain = picks(mains)
    taken = dot(pick, rows)
    if weighted:
        taken = taken * jnp.sum(gain, axis=1, keepdims=True)
    out_ref[:, : slots.width] = taken.astype(BF16)
    if slots.fold:
        taken = jnp.zeros((slots.total, LANES), F32)
        total_gain = jnp.zeros((slots.total, tokens), F32)
        for f in range(slots.blocks):
            pick, gain = picks([fold + float(f * slots.rem) for fold in folds])
            taken = taken + dot(pick, rows[:, f * LANES : (f + 1) * LANES])
            total_gain = total_gain + gain
        if weighted:
            taken = taken * jnp.sum(total_gain, axis=1, keepdims=True)
        out_ref[:, slots.width :] = taken.astype(BF16)


def dispatch(slots, weighted, ids, gains, rows):
    return pl.pallas_call(
        functools.partial(dispatch_kernel, slots, weighted),
        out_shape=jax.ShapeDtypeStruct((slots.total, slots.columns), BF16),
        compiler_params=pltpu.CompilerParams(vmem_limit_bytes=VMEM_BYTES),
        cost_estimate=cost(4 * slots.total * LANES * slots.width, 4 * slots.total * slots.columns),
        name="dispatch_scaled" if weighted else "dispatch_rows",
    )(ids, gains, rows)


def combine_kernel(slots, weighted, ids_ref, gain_ref, back_ref, out_ref):
    tokens, top = ids_ref.shape
    places = route_places(ids_ref[...], slots)
    slot = iota((tokens, slots.total), 1).astype(F32)

    def table(wanted):
        found = jnp.zeros((tokens, slots.total), F32)
        for r in range(top):
            value = gain_ref[:, r : r + 1] if weighted else 1.0
            found = jnp.where(slot == wanted[r], value, found)
        return found

    def apply(found, rows):
        high = found.astype(BF16)
        result = dot(high, rows)
        if weighted:
            result = result + dot((found - high.astype(F32)).astype(BF16), rows)
        return result

    result = apply(table([main for main, _ in places]), back_ref[:, : slots.width])
    if slots.fold:
        folded = back_ref[:, slots.width :]
        extra = [
            apply(table([start + float(f * slots.rem) for _, start in places]), folded)
            for f in range(slots.blocks)
        ]
        result = result + jnp.concatenate(extra, axis=1)
    out_ref[...] = result.astype(BF16)


def combine(slots, weighted, ids, gains, back):
    tokens = ids.shape[0]
    return pl.pallas_call(
        functools.partial(combine_kernel, slots, weighted),
        out_shape=jax.ShapeDtypeStruct((tokens, slots.width), BF16),
        compiler_params=pltpu.CompilerParams(vmem_limit_bytes=VMEM_BYTES),
        cost_estimate=cost(8 * slots.total * LANES * slots.width, 4 * slots.total * slots.columns),
        name="combine_out" if weighted else "combine_in",
    )(ids, gains, back)


def fold_table(slots, shape, folded_dim):
    folded = iota(shape, folded_dim)
    plain = iota(shape, 1 - folded_dim)
    rem_bits = int(math.log2(slots.rem))
    exp_bits = int(math.log2(slots.exp_count))
    j = plain & (slots.rem - 1)
    source = (plain >> rem_bits) & (slots.exp_count - 1)
    f = plain >> (rem_bits + exp_bits)
    return (folded == source * slots.rows + f * slots.rem + j).astype(F32).astype(BF16)


def unpack_rows(slots, block):
    flat = block.reshape(slots.exp_count * slots.rows, slots.columns)
    if not slots.fold:
        return flat
    each = slots.exp_count * slots.rem
    plain = dot(
        fold_table(slots, (slots.blocks * each, slots.exp_count * slots.rows), 1),
        flat[:, slots.width :],
    ).astype(BF16)
    extra = jnp.concatenate(
        [plain[f * each : (f + 1) * each] for f in range(slots.blocks)], axis=1
    )
    return jnp.concatenate([flat[:, : slots.width], extra], axis=0)


def pack_rows(slots, rows, out_ref):
    count = slots.exp_count * slots.rows
    main = rows[:count].reshape(slots.exp_count, 1, slots.rows, slots.width)
    out_ref[:, :, :, : slots.width] = main
    if slots.fold:
        each = slots.exp_count * slots.rem
        stacked = jnp.concatenate(
            [rows[count:, f * LANES : (f + 1) * LANES] for f in range(slots.blocks)], axis=0
        )
        folded = dot(fold_table(slots, (count, slots.blocks * each), 0), stacked).astype(BF16)
        out_ref[:, :, :, slots.width :] = folded.reshape(
            slots.exp_count, 1, slots.rows, LANES
        )


def ff_tile(width):
    return 256 if width % 256 == 0 else width


def gate_up_kernel(slots, pick_ref, recv_ref, gate_ref, up_ref, out_ref, rows_ref):
    @pl.when(pl.program_id(0) == 0)
    def _():
        rows_ref[...] = unpack_rows(slots, recv_ref[...])

    rows = rows_ref[...]
    out_ref[0] = dot(rows, gate_ref[0]).astype(out_ref.dtype)
    out_ref[1] = dot(rows, up_ref[0]).astype(out_ref.dtype)


def gate_up(slots, expert, recv, gate_proj, up_proj, dtype):
    local, width, ff = gate_proj.shape
    tile = ff_tile(ff)
    weights = pl.BlockSpec((1, width, tile), lambda i, e: (e[0], 0, i))
    return pl.pallas_call(
        functools.partial(gate_up_kernel, slots),
        grid_spec=pltpu.PrefetchScalarGridSpec(
            num_scalar_prefetch=1,
            grid=(ff // tile,),
            in_specs=[
                pl.BlockSpec(
                    (slots.exp_count, 1, slots.rows, slots.columns), lambda i, e: (0, e[0], 0, 0)
                ),
                weights,
                weights,
            ],
            out_specs=pl.BlockSpec((2, slots.per_expert, tile), lambda i, e: (0, 0, i)),
            scratch_shapes=[pltpu.VMEM((slots.per_expert, width), BF16)],
        ),
        out_shape=jax.ShapeDtypeStruct((2, slots.per_expert, ff), dtype),
        compiler_params=params(),
        cost_estimate=cost(4 * slots.per_expert * width * ff, 4 * width * ff),
        name="gate_up",
    )(expert, recv, gate_proj, up_proj)


def hidden_grad_kernel(slots, pick_ref, recv_ref, down_ref, out_ref, rows_ref):
    @pl.when(pl.program_id(0) == 0)
    def _():
        rows_ref[...] = unpack_rows(slots, recv_ref[...])

    out_ref[...] = dot(rows_ref[...], down_ref[0], 1, 1).astype(out_ref.dtype)


def hidden_grad_part(slots, expert, recv, down_proj, dtype):
    local, ff, width = down_proj.shape
    tile = ff_tile(ff)
    return pl.pallas_call(
        functools.partial(hidden_grad_kernel, slots),
        grid_spec=pltpu.PrefetchScalarGridSpec(
            num_scalar_prefetch=1,
            grid=(ff // tile,),
            in_specs=[
                pl.BlockSpec(
                    (slots.exp_count, 1, slots.rows, slots.columns), lambda i, e: (0, e[0], 0, 0)
                ),
                pl.BlockSpec((1, tile, width), lambda i, e: (e[0], i, 0)),
            ],
            out_specs=pl.BlockSpec((slots.per_expert, tile), lambda i, e: (0, i)),
            scratch_shapes=[pltpu.VMEM((slots.per_expert, width), BF16)],
        ),
        out_shape=jax.ShapeDtypeStruct((slots.per_expert, ff), dtype),
        compiler_params=params(),
        cost_estimate=cost(2 * slots.per_expert * width * ff, 2 * width * ff),
        name="hidden_grad",
    )(expert, recv, down_proj)


def route_out_kernel(slots, pick_ref, mine_ref, other_ref, down_ref, out_ref):
    hidden = jnp.where(pl.program_id(0) == 0, mine_ref[...], other_ref[...])
    pack_rows(slots, dot(hidden, down_ref[0]).astype(BF16), out_ref)


def route_out(slots, order, mine, other, down_proj):
    local, ff, width = down_proj.shape
    whole = pl.BlockSpec(mine.shape, lambda i, e: (0, 0))
    return pl.pallas_call(
        functools.partial(route_out_kernel, slots),
        grid_spec=pltpu.PrefetchScalarGridSpec(
            num_scalar_prefetch=1,
            grid=(local,),
            in_specs=[whole, whole, pl.BlockSpec((1, ff, width), lambda i, e: (e[i], 0, 0))],
            out_specs=pl.BlockSpec(
                (slots.exp_count, 1, slots.rows, slots.columns), lambda i, e: (0, e[i], 0, 0)
            ),
        ),
        out_shape=jax.ShapeDtypeStruct((slots.exp_count, local, slots.rows, slots.columns), BF16),
        compiler_params=params(),
        cost_estimate=cost(4 * slots.per_expert * width * ff, 4 * width * ff),
        name="route_out",
    )(order, mine, other, down_proj)


def route_in_kernel(slots, pick_ref, mine_ref, other_ref, gate_ref, up_ref, out_ref):
    first = pl.program_id(0) == 0
    gate_back = jnp.where(first, mine_ref[0], other_ref[0])
    up_back = jnp.where(first, mine_ref[1], other_ref[1])
    total = dot(gate_back, gate_ref[0], 1, 1) + dot(up_back, up_ref[0], 1, 1)
    pack_rows(slots, total.astype(BF16), out_ref)


def route_in(slots, order, mine, other, gate_proj, up_proj):
    local, width, ff = gate_proj.shape
    whole = pl.BlockSpec(mine.shape, lambda i, e: (0, 0, 0))
    weights = pl.BlockSpec((1, width, ff), lambda i, e: (e[i], 0, 0))
    return pl.pallas_call(
        functools.partial(route_in_kernel, slots),
        grid_spec=pltpu.PrefetchScalarGridSpec(
            num_scalar_prefetch=1,
            grid=(local,),
            in_specs=[whole, whole, weights, weights],
            out_specs=pl.BlockSpec(
                (slots.exp_count, 1, slots.rows, slots.columns), lambda i, e: (0, e[i], 0, 0)
            ),
        ),
        out_shape=jax.ShapeDtypeStruct((slots.exp_count, local, slots.rows, slots.columns), BF16),
        compiler_params=params(),
        cost_estimate=cost(8 * slots.per_expert * width * ff, 8 * width * ff),
        name="route_in",
    )(order, mine, other, gate_proj, up_proj)


def attention_kernel(
    offsets, tokens, chunk, me_ref, q_ref, g_ref, kv_ref, kv_far_ref,
    out_ref, qgrad_ref, keep_ref, send_ref,
    probs_ref, low_ref, key_t, value_t, key_acc, value_acc,
):
    d = HEAD_SIZE
    step = pl.program_id(0)
    me = me_ref[0]
    half = kv_ref.shape[0]
    seq = 2 * half
    scale = d ** (-0.5)
    to_base2 = scale * math.log2(math.e)

    @pl.when(step == 0)
    def _():
        for start, ref in ((0, kv_ref), (half, kv_far_ref)):
            for at in range(0, half, tokens):
                both = jnp.transpose(ref[at : at + tokens, :].astype(F32)).astype(BF16)
                key_t[:, start + at : start + at + tokens] = both[:d]
                value_t[:, start + at : start + at + tokens] = both[d:]
        key_acc[...] = jnp.zeros_like(key_acc)
        value_acc[...] = jnp.zeros_like(value_acc)

    def piece(at, first):
        ref, start = (kv_ref, at) if at < half else (kv_far_ref, at - half)
        return ref[start : start + chunk, first : first + d]

    heads = q_ref.shape[1] // d
    lanes = heads * tokens
    q = jnp.concatenate([q_ref[:, h * d : (h + 1) * d] for h in range(heads)], axis=0)
    g = jnp.concatenate([g_ref[:, h * d : (h + 1) * d] for h in range(heads)], axis=0)
    q_t = jnp.transpose(q.astype(F32)).astype(BF16)
    g_t32 = jnp.transpose(g.astype(F32))
    g_t = g_t32.astype(BF16)
    query_token = iota((tokens, lanes), 1) & (tokens - 1)
    key_token = iota((tokens, lanes), 0)
    ahead = key_token - query_token

    top = jnp.full((1, lanes), -jnp.inf, F32)
    for at in range(0, seq, chunk):
        scores = dot(piece(at, 0), q_t)
        for part in range(0, chunk, tokens):
            block = me ^ offsets[(at + part) // tokens]
            allowed = ahead <= (me - block) * tokens
            some = jnp.where(allowed, scores[part : part + tokens], -jnp.inf)
            probs_ref[at + part : at + part + tokens, :] = some
            top = jnp.maximum(top, jnp.max(some, axis=0, keepdims=True))
    top = top * to_base2
    total = jnp.zeros((1, lanes), F32)
    for at in range(0, seq, chunk):
        raised = jnp.exp2(probs_ref[at : at + chunk, :] * to_base2 - top)
        probs_ref[at : at + chunk, :] = raised
        total = total + jnp.sum(raised, axis=0, keepdims=True)
    inverse = 1.0 / total
    attended = jnp.zeros((d, lanes), F32)
    for at in range(0, seq, chunk):
        low = (probs_ref[at : at + chunk, :] * inverse).astype(BF16)
        low_ref[at : at + chunk, :] = low
        attended = attended + dot(value_t[:, at : at + chunk], low)
        value_acc[at : at + chunk, :] += dot(low, g)
    attended = attended.astype(BF16).astype(F32)
    row_dot = jnp.sum(g_t32 * attended, axis=0, keepdims=True)
    query_back = jnp.zeros((d, lanes), F32)
    for at in range(0, seq, chunk):
        prob_grad = dot(piece(at, d), g_t)
        score_grad = (low_ref[at : at + chunk, :].astype(F32) * (prob_grad - row_dot)).astype(BF16)
        query_back = query_back + dot(key_t[:, at : at + chunk], score_grad)
        key_acc[at : at + chunk, :] += dot(score_grad, q)
    for h in range(heads):
        rows = slice(h * tokens, (h + 1) * tokens)
        out_ref[:, h * d : (h + 1) * d] = jnp.transpose(attended[:, rows]).astype(BF16)
        qgrad_ref[:, h * d : (h + 1) * d] = jnp.transpose(query_back[:, rows] * scale).astype(BF16)

    @pl.when(step == pl.num_programs(0) - 1)
    def _():
        keep_ref[:, :d] = key_acc[:half, :] * scale
        keep_ref[:, d:] = value_acc[:half, :]
        send_ref[:, :d] = (key_acc[half:, :] * scale).astype(BF16)
        send_ref[:, d:] = value_acc[half:, :].astype(BF16)


def attention(me, offsets, queries, attn_grad, kv_near, kv_far):
    tokens, columns = queries.shape
    half, both = kv_near.shape
    seq = 2 * half
    heads = columns // HEAD_SIZE
    group = 2 if heads % 2 == 0 else 1
    lanes = group * tokens
    chunk = min(256, half)
    tile = pl.BlockSpec((tokens, group * HEAD_SIZE), lambda i, m: (0, i))
    whole = pl.BlockSpec((half, both), lambda i, m: (0, 0))
    return pl.pallas_call(
        functools.partial(attention_kernel, offsets, tokens, chunk),
        grid_spec=pltpu.PrefetchScalarGridSpec(
            num_scalar_prefetch=1,
            grid=(heads // group,),
            in_specs=[tile, tile, whole, whole],
            out_specs=[tile, tile, whole, whole],
            scratch_shapes=[
                pltpu.VMEM((seq, lanes), F32),
                pltpu.VMEM((seq, lanes), BF16),
                pltpu.VMEM((HEAD_SIZE, seq), BF16),
                pltpu.VMEM((HEAD_SIZE, seq), BF16),
                pltpu.VMEM((seq, HEAD_SIZE), F32),
                pltpu.VMEM((seq, HEAD_SIZE), F32),
            ],
        ),
        out_shape=[
            jax.ShapeDtypeStruct(queries.shape, BF16),
            jax.ShapeDtypeStruct(queries.shape, BF16),
            jax.ShapeDtypeStruct((half, both), F32),
            jax.ShapeDtypeStruct((half, both), BF16),
        ],
        compiler_params=params(),
        cost_estimate=cost(12 * tokens * columns * seq, 8 * tokens * columns, tokens * heads * seq),
        name="attention",
    )(me, queries, attn_grad, kv_near, kv_far)


def swap(value, axis, bit):
    count = lax.axis_size(axis)
    return lax.ppermute(value, axis, [(i, i ^ bit) for i in range(count)])


def far_bits(count):
    bits = []
    bit = count // 2
    while bit >= 1:
        bits.append(bit)
        bit //= 2
    return bits


def spread_sum(part, ctx_count):
    bit = 2
    while bit < ctx_count:
        part = part + swap(part.astype(BF16), "ctx", bit).astype(F32)
        bit *= 2
    return part


def activate(gate, up):
    return (jax.nn.silu(gate) * up).astype(BF16)


def gate_backward(hidden_grad, gate, up):
    s = jax.nn.sigmoid(gate)
    gate_back = (hidden_grad * up * s * (1.0 + gate * (1.0 - s))).astype(BF16)
    up_back = (hidden_grad * (gate * s)).astype(BF16)
    return jnp.stack([gate_back, up_back])


def body(
    queries, key_proj, value_matrix_rows, attn_grad, moe_input, moe_grad,
    expert_ids, route_weights, gate_proj, up_proj, down_proj,
):
    ctx_count = lax.axis_size("ctx")
    exp_count = lax.axis_size("exp")
    ctx_index = lax.axis_index("ctx")
    exp_index = lax.axis_index("exp")
    tokens = queries.shape[0]
    d = HEAD_SIZE
    kv_heads = key_proj.shape[1] // d
    sharers = ctx_count // kv_heads
    kv_head = ctx_index // sharers
    width = moe_input.shape[1]
    local = gate_proj.shape[0]
    expert_total = local * exp_count
    slot_count = 2 * ((tokens + expert_total - 2) // (expert_total - 1))
    slots = Slots(slot_count, width, exp_count, local)
    core = ctx_index % 2
    mine = core.astype(jnp.int32).reshape(1)
    other = 1 - mine
    order = jnp.concatenate([mine, other])
    shape = (exp_count, local, slots.rows, slots.columns)

    def exchange(rows):
        flat = rows.reshape(exp_count, local * slots.rows, slots.columns)
        return lax.all_to_all(flat, "exp", split_axis=0, concat_axis=0, tiled=True)

    kv = jnp.concatenate(
        [
            lax.dynamic_slice_in_dim(key_proj, kv_head * d, d, 1),
            lax.dynamic_slice_in_dim(value_matrix_rows, kv_head * d, d, 1),
        ],
        axis=1,
    )
    offsets = [0]
    kv_far = None
    for bit in far_bits(exp_count):
        if kv_far is not None:
            kv = jnp.concatenate([kv, kv_far], axis=0)
        kv_far = swap(kv, "exp", bit)
        offsets = offsets + [o ^ bit for o in offsets]

    send_rows = dispatch(slots, False, expert_ids, route_weights, moe_input)
    recv_rows = exchange(send_rows).reshape(shape)
    send_scaled = dispatch(slots, True, expert_ids, route_weights, moe_grad)
    recv_scaled = exchange(send_scaled).reshape(shape)

    attn_out, query_grad, kv_keep, kv_send = attention(
        exp_index.astype(jnp.int32).reshape(1), tuple(offsets), queries, attn_grad, kv, kv_far
    )

    gu_send = gate_up(slots, other, recv_rows, gate_proj, up_proj, BF16)
    gu_recv = swap(gu_send, "ctx", 1)
    gu_keep = gate_up(slots, mine, recv_rows, gate_proj, up_proj, F32)
    gate_full, up_full = spread_sum(gu_keep + gu_recv.astype(F32), ctx_count)
    hidden = activate(gate_full, up_full)
    hidden_other = swap(hidden, "ctx", 1)
    out_rows = route_out(slots, order, hidden, hidden_other, down_proj)
    back_out = exchange(out_rows).reshape(slots.total, slots.columns)

    hg_send = hidden_grad_part(slots, other, recv_scaled, down_proj, BF16)
    hg_recv = swap(hg_send, "ctx", 1)
    hg_keep = hidden_grad_part(slots, mine, recv_scaled, down_proj, F32)
    hg_full = spread_sum(hg_keep + hg_recv.astype(F32), ctx_count)
    back = gate_backward(hg_full, gate_full, up_full)
    back_other = swap(back, "ctx", 1)
    in_rows = route_in(slots, order, back, back_other, gate_proj, up_proj)
    back_in = exchange(in_rows).reshape(slots.total, slots.columns)

    moe_out = combine(slots, True, expert_ids, route_weights, back_out)
    input_grad = combine(slots, False, expert_ids, route_weights, back_in)

    kv_sum = kv_keep
    for bit in reversed(far_bits(exp_count)):
        kv_sum = kv_sum + swap(kv_send, "exp", bit).astype(F32)
        half = kv_sum.shape[0] // 2
        if bit != exp_count // 2:
            kv_send = kv_sum[half:].astype(BF16)
            kv_sum = kv_sum[:half]
    kv_every = lax.all_gather(kv_sum.astype(BF16), "ctx", axis=0, tiled=False)
    if sharers > 1:
        kv_every = kv_every.astype(F32).reshape(kv_heads, sharers, tokens, 2 * d).sum(axis=1)
    kv_every = kv_every.astype(BF16)
    key_grad = jnp.concatenate([kv_every[h, :, :d] for h in range(kv_heads)], axis=1)
    value_grad = jnp.concatenate([kv_every[h, :, d:] for h in range(kv_heads)], axis=1)
    return (attn_out, query_grad, key_grad, value_grad, moe_out, input_grad)


def solution(mesh):
    placed = (
        P("exp", "ctx"),
        P("exp", None),
        P("exp", None),
        P("exp", "ctx"),
        P("exp", "ctx"),
        P("exp", "ctx"),
        P("exp", None),
        P("exp", None),
        P("exp", "ctx", None),
        P("exp", "ctx", None),
        P("exp", None, "ctx"),
    )
    return jax.shard_map(
        body,
        mesh=mesh,
        in_specs=placed,
        out_specs=(
            P("exp", "ctx"),
            P("exp", "ctx"),
            P("exp", None),
            P("exp", None),
            P("exp", "ctx"),
            P("exp", "ctx"),
        ),
        check_vma=False,
    )
```

```python
import functools
import math

import jax
import jax.numpy as jnp
from jax import lax
from jax.experimental import pallas as pl
from jax.experimental.pallas import tpu as pltpu
from jax.sharding import PartitionSpec as P

HEAD_SIZE = 128
LANES = 128
ROW_TILE = 16
PAIRS = 2
SMALL_VMEM = 16 * 1024 * 1024
LARGE_VMEM = 20 * 1024 * 1024
EXPERT_VMEM = 16 * 1024 * 1024
BF16 = jnp.bfloat16
F32 = jnp.float32


def dot(a, b, a_dim=1, b_dim=0):
    return lax.dot_general(a, b, (((a_dim,), (b_dim,)), ((), ())), preferred_element_type=F32)


def iota(shape, dim):
    return lax.broadcasted_iota(jnp.int32, shape, dim)


def params(vmem_bytes):
    return pltpu.CompilerParams(vmem_limit_bytes=vmem_bytes, dimension_semantics=("arbitrary",))


def in_hbm(value):
    return pltpu.with_memory_space_constraint(value, pltpu.HBM)


def cost(flops, bytes_accessed, transcendentals=0):
    return pl.CostEstimate(
        flops=int(flops), bytes_accessed=int(bytes_accessed), transcendentals=int(transcendentals)
    )


def power_of_two(value):
    return value > 0 and value & (value - 1) == 0


class Slots:
    def __init__(self, slot_count, width, exp_count, local_experts):
        whole = slot_count // ROW_TILE * ROW_TILE
        rem = slot_count - whole
        blocks = width // LANES
        self.fold = (
            whole > 0
            and rem > 0
            and power_of_two(rem)
            and power_of_two(exp_count)
            and rem * blocks <= whole
            and (rem * exp_count) % ROW_TILE == 0
        )
        self.rows = whole if self.fold or rem == 0 else whole + ROW_TILE
        self.rem = rem if self.fold else 0
        self.blocks = blocks
        self.width = width
        self.columns = width + (LANES if self.fold else 0)
        self.exp_count = exp_count
        self.local = local_experts
        self.experts = exp_count * local_experts
        self.total = self.experts * self.rows
        self.per_expert = exp_count * (self.rows + self.rem)


def route_places(ids, slots):
    top, tokens = ids.shape
    expert = iota((-(-slots.experts // ROW_TILE) * ROW_TILE, tokens), 0)
    hits = [(ids[r : r + 1, :] == expert).astype(F32) for r in range(top)]
    earlier = (iota((tokens, tokens), 0) < iota((tokens, tokens), 1)).astype(BF16)
    before = dot(sum(hits).astype(BF16), earlier)
    found = []
    for r in range(top):
        rank = jnp.sum(hits[r] * before, axis=0, keepdims=True)
        base = ids[r : r + 1, :].astype(F32) * slots.rows
        inside = rank < slots.rows
        main = jnp.where(inside, base + rank, -1.0)
        folded = jnp.where(inside, -65536.0, base + rank - slots.rows)
        found.append((main, folded))
    return found


def as_column(row):
    tokens = row.shape[1]
    return jnp.transpose(jnp.broadcast_to(row, (LANES, tokens)))[:, 0:1]


def dispatch_kernel(slots, weighted, ids_ref, gain_ref, rows_ref, out_ref):
    top, tokens = ids_ref.shape
    places = route_places(ids_ref[...], slots)
    gains = [gain_ref[r : r + 1, :] for r in range(top)]
    slot = iota((slots.total, tokens), 0).astype(F32)
    rows = rows_ref[...]

    def picks(wanted):
        pick = jnp.zeros((slots.total, tokens), F32)
        gain = pick
        for r in range(top):
            here = slot == wanted[r]
            pick = jnp.where(here, 1.0, pick)
            gain = jnp.where(here, gains[r], gain)
        return pick.astype(BF16), gain

    pick, gain = picks([main for main, _ in places])
    taken = dot(pick, rows)
    if weighted:
        taken = taken * jnp.sum(gain, axis=1, keepdims=True)
    out_ref[:, : slots.width] = taken.astype(BF16)
    if slots.fold:
        taken = jnp.zeros((slots.total, LANES), F32)
        total_gain = jnp.zeros((slots.total, tokens), F32)
        for f in range(slots.blocks):
            pick, gain = picks([start + float(f * slots.rem) for _, start in places])
            taken = taken + dot(pick, rows[:, f * LANES : (f + 1) * LANES])
            total_gain = total_gain + gain
        if weighted:
            taken = taken * jnp.sum(total_gain, axis=1, keepdims=True)
        out_ref[:, slots.width :] = taken.astype(BF16)


def dispatch(slots, weighted, ids, gains, rows):
    return pl.pallas_call(
        functools.partial(dispatch_kernel, slots, weighted),
        out_shape=jax.ShapeDtypeStruct((slots.total, slots.columns), BF16),
        compiler_params=pltpu.CompilerParams(vmem_limit_bytes=LARGE_VMEM),
        cost_estimate=cost(4 * slots.total * LANES * slots.width, 4 * slots.total * slots.columns),
        name="dispatch_scaled" if weighted else "dispatch_rows",
    )(in_hbm(ids), in_hbm(gains), in_hbm(rows))


def combine_kernel(slots, weighted, ids_ref, gain_ref, back_ref, out_ref):
    top, tokens = ids_ref.shape
    places = [
        (as_column(main), as_column(start))
        for main, start in route_places(ids_ref[...], slots)
    ]
    gains = [as_column(gain_ref[r : r + 1, :]) if weighted else 1.0 for r in range(top)]
    slot = iota((tokens, slots.total), 1).astype(F32)

    def table(wanted):
        found = jnp.zeros((tokens, slots.total), F32)
        for r in range(top):
            found = jnp.where(slot == wanted[r], gains[r], found)
        return found

    def apply(found, rows):
        high = found.astype(BF16)
        result = dot(high, rows)
        if weighted:
            result = result + dot((found - high.astype(F32)).astype(BF16), rows)
        return result

    result = apply(table([main for main, _ in places]), back_ref[:, : slots.width])
    if slots.fold:
        folded = back_ref[:, slots.width :]
        extra = [
            apply(table([start + float(f * slots.rem) for _, start in places]), folded)
            for f in range(slots.blocks)
        ]
        result = result + jnp.concatenate(extra, axis=1)
    out_ref[...] = result.astype(BF16)


def combine(slots, weighted, ids, gains, back):
    tokens = ids.shape[1]
    return pl.pallas_call(
        functools.partial(combine_kernel, slots, weighted),
        out_shape=jax.ShapeDtypeStruct((tokens, slots.width), BF16),
        compiler_params=pltpu.CompilerParams(vmem_limit_bytes=SMALL_VMEM),
        cost_estimate=cost(8 * slots.total * LANES * slots.width, 4 * slots.total * slots.columns),
        name="combine_out" if weighted else "combine_in",
    )(ids, gains, back)


def fold_table(slots, shape, folded_dim):
    folded = iota(shape, folded_dim)
    plain = iota(shape, 1 - folded_dim)
    rem_bits = int(math.log2(slots.rem))
    exp_bits = int(math.log2(slots.exp_count))
    j = plain & (slots.rem - 1)
    source = (plain >> rem_bits) & (slots.exp_count - 1)
    f = plain >> (rem_bits + exp_bits)
    return (folded == source * slots.rows + f * slots.rem + j).astype(F32).astype(BF16)


def unpack_rows(slots, block):
    flat = block.reshape(slots.exp_count * slots.rows, slots.columns)
    if not slots.fold:
        return flat
    each = slots.exp_count * slots.rem
    plain = dot(
        fold_table(slots, (slots.blocks * each, slots.exp_count * slots.rows), 1),
        flat[:, slots.width :],
    ).astype(BF16)
    extra = jnp.concatenate(
        [plain[f * each : (f + 1) * each] for f in range(slots.blocks)], axis=1
    )
    return jnp.concatenate([flat[:, : slots.width], extra], axis=0)


def pack_rows(slots, rows, out_ref):
    count = slots.exp_count * slots.rows
    main = rows[:count].reshape(slots.exp_count, slots.rows, slots.width)
    out_ref[:, :, : slots.width] = main
    if slots.fold:
        each = slots.exp_count * slots.rem
        stacked = jnp.concatenate(
            [rows[count:, f * LANES : (f + 1) * LANES] for f in range(slots.blocks)], axis=0
        )
        folded = dot(fold_table(slots, (count, slots.blocks * each), 0), stacked).astype(BF16)
        out_ref[:, :, slots.width :] = folded.reshape(slots.exp_count, slots.rows, LANES)


def hold_kernel(*refs):
    count = len(refs) // 2
    copies = [
        pltpu.make_async_copy(refs[i], refs[count + i], refs[-1].at[i]) for i in range(count)
    ]
    for copy in copies:
        copy.start()
    for copy in copies:
        copy.wait()


def hold(*weights):
    return pl.pallas_call(
        hold_kernel,
        in_specs=[pl.BlockSpec(memory_space=pl.ANY)] * len(weights),
        out_specs=[pl.BlockSpec(memory_space=pltpu.VMEM)] * len(weights),
        out_shape=[pltpu.VMEM(value.shape, value.dtype) for value in weights],
        scratch_shapes=[pltpu.SemaphoreType.DMA((len(weights),))],
        compiler_params=pltpu.CompilerParams(vmem_limit_bytes=SMALL_VMEM),
        cost_estimate=cost(0, sum(value.size * 4 for value in weights)),
        name="hold_weights",
    )(*[in_hbm(value) for value in weights])


def expert_call(kernel, name, out_shape, scalars, *operands):
    in_vmem = pl.BlockSpec(memory_space=pltpu.VMEM)
    return pl.pallas_call(
        kernel,
        in_specs=[pl.BlockSpec(memory_space=pltpu.SMEM)] + [in_vmem] * len(operands),
        out_specs=[in_vmem] * len(out_shape) if isinstance(out_shape, list) else in_vmem,
        out_shape=out_shape,
        compiler_params=pltpu.CompilerParams(vmem_limit_bytes=EXPERT_VMEM),
        name=name,
    )(scalars, *operands)


def expert_part(kernel, name, slots, expert, recv, weights, shape, arrived):
    if arrived is None:
        out = jax.ShapeDtypeStruct(shape, BF16)
        return expert_call(functools.partial(kernel, slots), name, out, expert, recv, *weights)
    out = [jax.ShapeDtypeStruct(shape, F32), jax.ShapeDtypeStruct(shape, BF16)]
    return expert_call(functools.partial(kernel, slots), name, out, expert, recv, *weights, arrived)


def store_part(index, part, refs):
    if len(refs) == 1:
        refs[0][index] = part.astype(BF16)
        return
    arrived_ref, out_ref, low_ref = refs
    total = part + arrived_ref[index].astype(F32)
    out_ref[index] = total
    low_ref[index] = total.astype(BF16)


def gate_up_kernel(slots, expert_ref, recv_ref, gate_ref, up_ref, *refs):
    e = expert_ref[0]
    rows = unpack_rows(slots, recv_ref[:, e])
    store_part(0, dot(rows, gate_ref[e]), refs)
    store_part(1, dot(rows, up_ref[e]), refs)


def gate_up(slots, expert, recv, gate_proj, up_proj, arrived=None):
    shape = (2, slots.per_expert, gate_proj.shape[2])
    weights = (gate_proj, up_proj)
    return expert_part(gate_up_kernel, "gate_up", slots, expert, recv, weights, shape, arrived)


def hidden_grad_kernel(slots, expert_ref, recv_ref, down_ref, *refs):
    e = expert_ref[0]
    rows = unpack_rows(slots, recv_ref[:, e])
    store_part(..., dot(rows, down_ref[e], 1, 1), refs)


def hidden_grad_part(slots, expert, recv, down_proj, arrived=None):
    shape = (slots.per_expert, down_proj.shape[1])
    return expert_part(
        hidden_grad_kernel, "hidden_grad", slots, expert, recv, (down_proj,), shape, arrived
    )


def route_out_kernel(slots, order_ref, mine_ref, other_ref, down_ref, out_ref):
    for at, hidden_ref in enumerate((mine_ref, other_ref)):
        e = order_ref[at]
        pack_rows(slots, dot(hidden_ref[...], down_ref[e]).astype(BF16), out_ref.at[:, e])


def route_out(slots, order, mine, other, down_proj):
    out = jax.ShapeDtypeStruct((slots.exp_count, slots.local, slots.rows, slots.columns), BF16)
    kernel = functools.partial(route_out_kernel, slots)
    return expert_call(kernel, "route_out", out, order, mine, other, down_proj)


def route_in_kernel(slots, order_ref, mine_ref, other_ref, gate_ref, up_ref, out_ref):
    for at, back_ref in enumerate((mine_ref, other_ref)):
        e = order_ref[at]
        total = dot(back_ref[0], gate_ref[e], 1, 1) + dot(back_ref[1], up_ref[e], 1, 1)
        pack_rows(slots, total.astype(BF16), out_ref.at[:, e])


def route_in(slots, order, mine, other, gate_proj, up_proj):
    out = jax.ShapeDtypeStruct((slots.exp_count, slots.local, slots.rows, slots.columns), BF16)
    kernel = functools.partial(route_in_kernel, slots)
    return expert_call(kernel, "route_in", out, order, mine, other, gate_proj, up_proj)


def attention_kernel(offsets, tokens, chunk, first, last, me_ref, q_ref, g_ref, kv_ref, kv_far_ref, *refs):
    if not first:
        carry_ref, refs = refs[0], refs[3:]
    out_ref, qgrad_ref = refs[:2]
    if last:
        keep_ref, send_ref = refs[2:4]
    else:
        carried_ref = refs[2]
    scores_ref, low_ref, key_t, value_t, key_acc, value_acc = refs[-6:]
    d = HEAD_SIZE
    step = pl.program_id(0)
    me = me_ref[0]
    half = kv_ref.shape[0]
    seq = 2 * half
    scale = d ** (-0.5)
    to_base2 = scale * math.log2(math.e)

    @pl.when(step == 0)
    def _():
        for start, ref in ((0, kv_ref), (half, kv_far_ref)):
            for at in range(0, half, tokens):
                both = jnp.transpose(ref[at : at + tokens, :])
                key_t[:, start + at : start + at + tokens] = both[:d]
                value_t[:, start + at : start + at + tokens] = both[d:]
        if first:
            key_acc[...] = jnp.zeros_like(key_acc)
            value_acc[...] = jnp.zeros_like(value_acc)
        else:
            key_acc[...] = carry_ref[:, :d]
            value_acc[...] = carry_ref[:, d:]

    def piece(at, column):
        ref, start = (kv_ref, at) if at < half else (kv_far_ref, at - half)
        return ref[start : start + chunk, column : column + d]

    pairs = scores_ref.shape[0]
    lanes = scores_ref.shape[2]
    heads = lanes // tokens
    chunks = range(0, seq, chunk)
    ahead = iota((tokens, lanes), 0) - (iota((tokens, lanes), 1) & (tokens - 1))
    limits = [(me - (me ^ offset)) * tokens for offset in offsets]

    def columns(pair, h):
        start = (pair * heads + h) * d
        return slice(start, start + d)

    def stacked(ref, pair):
        return jnp.concatenate([ref[:, columns(pair, h)] for h in range(heads)], axis=0)

    every = range(pairs)
    q = [stacked(q_ref, pair) for pair in every]
    g = [stacked(g_ref, pair) for pair in every]
    q_t = [jnp.transpose(value) for value in q]
    g_t = [jnp.transpose(value) for value in g]

    top = []
    for pair in every:
        largest = jnp.full((1, lanes), -jnp.inf, F32)
        for at in chunks:
            scores = dot(piece(at, 0), q_t[pair])
            for part in range(0, chunk, tokens):
                allowed = ahead <= limits[(at + part) // tokens]
                some = jnp.where(allowed, scores[part : part + tokens], -jnp.inf)
                scores_ref[pair, at + part : at + part + tokens, :] = some
                largest = jnp.maximum(largest, jnp.max(some, axis=0, keepdims=True))
        top.append(largest * to_base2)
    inverse = []
    for pair in every:
        total = jnp.zeros((1, lanes), F32)
        for at in chunks:
            raised = jnp.exp2(scores_ref[pair, at : at + chunk, :] * to_base2 - top[pair])
            low_ref[pair, at : at + chunk, :] = raised.astype(BF16)
            total = total + jnp.sum(raised, axis=0, keepdims=True)
        inverse.append(1.0 / total)
    row_dot = []
    for pair in every:
        spread = jnp.zeros((d, lanes), F32)
        for at in chunks:
            spread = spread + dot(value_t[:, at : at + chunk], low_ref[pair, at : at + chunk, :])
        attended = (spread * inverse[pair]).astype(BF16).astype(F32)
        row_dot.append(jnp.sum(g_t[pair].astype(F32) * attended, axis=0, keepdims=True))
        for h in range(heads):
            rows = slice(h * tokens, (h + 1) * tokens)
            out_ref[:, columns(pair, h)] = jnp.transpose(attended[:, rows]).astype(BF16)
    for pair in every:
        q_even = jnp.transpose(q_t[pair].astype(F32) * inverse[pair]).astype(BF16)
        g_even = jnp.transpose(g_t[pair].astype(F32) * inverse[pair]).astype(BF16)
        query_back = jnp.zeros((d, lanes), F32)
        for at in chunks:
            low = low_ref[pair, at : at + chunk, :]
            prob_grad = dot(piece(at, d), g_t[pair])
            score_grad = (low.astype(F32) * (prob_grad - row_dot[pair])).astype(BF16)
            query_back = query_back + dot(key_t[:, at : at + chunk], score_grad)
            key_acc[at : at + chunk, :] += dot(score_grad, q_even)
            value_acc[at : at + chunk, :] += dot(low, g_even)
        query_back = query_back * (inverse[pair] * scale)
        for h in range(heads):
            rows = slice(h * tokens, (h + 1) * tokens)
            qgrad_ref[:, columns(pair, h)] = jnp.transpose(query_back[:, rows]).astype(BF16)

    @pl.when(step == pl.num_programs(0) - 1)
    def _():
        if last:
            keep_ref[:, :d] = key_acc[:half, :] * scale
            keep_ref[:, d:] = value_acc[:half, :]
            send_ref[:, :d] = (key_acc[half:, :] * scale).astype(BF16)
            send_ref[:, d:] = value_acc[half:, :].astype(BF16)
        else:
            carried_ref[:, :d] = key_acc[...]
            carried_ref[:, d:] = value_acc[...]


def attention(me, offsets, queries, attn_grad, kv_near, kv_far, part, parts, carried=None):
    tokens, columns = queries.shape
    half, both = kv_near.shape
    seq = 2 * half
    heads = columns // HEAD_SIZE
    group = 2 if heads % (2 * parts) == 0 else 1
    pairs = PAIRS if heads % (group * PAIRS * parts) == 0 and seq <= 2048 else 1
    lanes = group * tokens
    chunk = min(256, half)
    steps = heads // (group * pairs * parts)
    first, last = part == 0, part == parts - 1
    tile = pl.BlockSpec((tokens, pairs * group * HEAD_SIZE), lambda i, m: (0, i + part * steps))
    whole = pl.BlockSpec((half, both), lambda i, m: (0, 0))
    sums = pl.BlockSpec((seq, both), lambda i, m: (0, 0))
    held = pl.BlockSpec(memory_space=pl.ANY)
    wide = jax.ShapeDtypeStruct(queries.shape, BF16)
    if last:
        final = [jax.ShapeDtypeStruct((half, both), F32), jax.ShapeDtypeStruct((half, both), BF16)]
    else:
        final = [jax.ShapeDtypeStruct((seq, both), F32)]
    return pl.pallas_call(
        functools.partial(attention_kernel, offsets, tokens, chunk, first, last),
        grid_spec=pltpu.PrefetchScalarGridSpec(
            num_scalar_prefetch=1,
            grid=(steps,),
            in_specs=[tile, tile, whole, whole] + ([] if first else [sums, held, held]),
            out_specs=[tile, tile] + ([whole, whole] if last else [sums]),
            scratch_shapes=[
                pltpu.VMEM((pairs, seq, lanes), F32),
                pltpu.VMEM((pairs, seq, lanes), BF16),
                pltpu.VMEM((HEAD_SIZE, seq), BF16),
                pltpu.VMEM((HEAD_SIZE, seq), BF16),
                pltpu.VMEM((seq, HEAD_SIZE), F32),
                pltpu.VMEM((seq, HEAD_SIZE), F32),
            ],
        ),
        out_shape=[wide, wide] + final,
        input_output_aliases={} if first else {6: 0, 7: 1},
        compiler_params=params(LARGE_VMEM),
        cost_estimate=cost(
            12 * tokens * columns * seq // parts,
            8 * tokens * columns // parts,
            tokens * heads * seq // parts,
        ),
        name="attention",
    )(me, in_hbm(queries), in_hbm(attn_grad), kv_near, kv_far, *(() if first else (carried[2], carried[0], carried[1])))


def swap(value, axis, bit):
    count = lax.axis_size(axis)
    return lax.ppermute(value, axis, [(i, i ^ bit) for i in range(count)])


def after(value, *earlier):
    return lax.optimization_barrier((value, *earlier))[0]


def far_bits(count):
    bits = []
    bit = count // 2
    while bit >= 1:
        bits.append(bit)
        bit //= 2
    return bits


def spread_sum(part, low, ctx_count, beside):
    result = None
    bit = 2
    while bit < ctx_count:
        arrived = swap(low, "ctx", bit)
        if result is None:
            result = beside(low)
            arrived = after(arrived, *result)
        part = part + arrived.astype(F32)
        low = part.astype(BF16)
        bit *= 2
    return part, beside(low) if result is None else result


def activate(gate, up):
    return (jax.nn.silu(gate) * up).astype(BF16)


def gate_backward(hidden_grad, gate, up):
    s = jax.nn.sigmoid(gate)
    gate_back = (hidden_grad * up * s * (1.0 + gate * (1.0 - s))).astype(BF16)
    up_back = (hidden_grad * (gate * s)).astype(BF16)
    return jnp.stack([gate_back, up_back])


def body(
    queries, key_proj, value_matrix_rows, attn_grad, moe_input, moe_grad,
    expert_ids, route_weights, gate_proj, up_proj, down_proj,
):
    ctx_count = lax.axis_size("ctx")
    exp_count = lax.axis_size("exp")
    ctx_index = lax.axis_index("ctx")
    exp_index = lax.axis_index("exp")
    tokens = queries.shape[0]
    d = HEAD_SIZE
    kv_heads = key_proj.shape[1] // d
    sharers = ctx_count // kv_heads
    kv_head = ctx_index // sharers
    width = moe_input.shape[1]
    local = gate_proj.shape[0]
    expert_total = local * exp_count
    slot_count = 2 * ((tokens + expert_total - 2) // (expert_total - 1))
    slots = Slots(slot_count, width, exp_count, local)
    core = ctx_index % 2
    mine = core.astype(jnp.int32).reshape(1)
    other = 1 - mine
    order = jnp.concatenate([mine, other])
    shape = (exp_count, local, slots.rows, slots.columns)

    def exchange(rows):
        flat = rows.reshape(exp_count, local * slots.rows, slots.columns)
        return lax.all_to_all(flat, "exp", split_axis=0, concat_axis=0, tiled=True)

    me = exp_index.astype(jnp.int32).reshape(1)
    ids = expert_ids.T
    gains = route_weights.T
    send_rows = dispatch(slots, False, ids, gains, moe_input)
    recv_rows = exchange(send_rows).reshape(shape)
    send_scaled = dispatch(slots, True, ids, gains, after(moe_grad, send_rows))

    key_proj = after(key_proj, send_scaled)
    own = jnp.concatenate(
        [
            lax.dynamic_slice_in_dim(key_proj, kv_head * d, d, 1),
            lax.dynamic_slice_in_dim(value_matrix_rows, kv_head * d, d, 1),
        ],
        axis=1,
    )
    offsets = list(range(0, exp_count, 2)) + list(range(1, exp_count, 2))
    gathered = [swap(own, "exp", offset) for offset in offsets[1 : exp_count // 2]]
    gate_held, up_held, down_proj = hold(after(gate_proj, own), up_proj, down_proj)
    kv = jnp.concatenate([own, *gathered], axis=0)
    kv_far = swap(kv, "exp", 1)

    def heads(part, carried, earlier):
        return attention(
            me, tuple(offsets), after(queries, earlier), attn_grad, kv, kv_far, part, 1, carried
        )

    recv_rows = after(recv_rows, down_proj)
    gu_send = gate_up(slots, other, recv_rows, gate_held, up_held)
    gu_recv = swap(gu_send, "ctx", 1)
    recv_rows = after(recv_rows, gu_send, kv)
    gu_part, gu_low = gate_up(slots, mine, recv_rows, gate_held, up_held, gu_recv)
    recv_scaled = exchange(after(send_scaled, gu_low)).reshape(shape)
    (gate_full, up_full), (attn_out, query_grad, kv_keep, kv_send) = spread_sum(
        gu_part, gu_low, ctx_count, lambda part: heads(0, None, part)
    )
    hidden = activate(gate_full, up_full)
    hidden_other = swap(hidden, "ctx", 1)
    hg_send = hidden_grad_part(slots, other, after(recv_scaled, hidden), down_proj)
    hg_recv = swap(hg_send, "ctx", 1)
    out_rows = route_out(slots, order, after(hidden, hg_send), hidden_other, down_proj)
    back_out = exchange(out_rows).reshape(slots.total, slots.columns)

    hg_part, hg_low = hidden_grad_part(
        slots, mine, after(recv_scaled, out_rows), down_proj, hg_recv
    )
    hg_full, _ = spread_sum(hg_part, hg_low, ctx_count, lambda part: (part,))
    kv_sum = kv_keep + swap(kv_send, "exp", 1).astype(F32)
    kv_low = kv_sum.astype(BF16)
    blocks = exp_count // 2
    kv_parts = [
        swap(kv_low[i * tokens : (i + 1) * tokens], "exp", offsets[i]) for i in range(1, blocks)
    ]
    back = gate_backward(hg_full, gate_full, up_full)
    back_other = swap(back, "ctx", 1)
    kv_total = kv_sum[:tokens]
    for part in kv_parts:
        kv_total = kv_total + part.astype(F32)
    kv_total = kv_total.astype(BF16)
    in_rows = route_in(slots, order, back, back_other, gate_proj, up_proj)
    back_in = exchange(after(in_rows, kv_total)).reshape(slots.total, slots.columns)

    moe_out = combine(slots, True, ids, gains, after(back_out, in_rows))
    input_grad = combine(slots, False, ids, gains, back_in)

    kv_every = lax.all_gather(after(kv_total, in_rows), "ctx", axis=0, tiled=False)
    if sharers > 1:
        kv_every = kv_every.astype(F32).reshape(kv_heads, sharers, tokens, 2 * d).sum(axis=1)
    kv_every = kv_every.astype(BF16)
    key_grad = jnp.concatenate([kv_every[h, :, :d] for h in range(kv_heads)], axis=1)
    value_grad = jnp.concatenate([kv_every[h, :, d:] for h in range(kv_heads)], axis=1)
    return (attn_out, query_grad, key_grad, value_grad, moe_out, input_grad)


def solution(mesh):
    placed = (
        P("exp", "ctx"),
        P("exp", None),
        P("exp", None),
        P("exp", "ctx"),
        P("exp", "ctx"),
        P("exp", "ctx"),
        P("exp", None),
        P("exp", None),
        P("exp", "ctx", None),
        P("exp", "ctx", None),
        P("exp", None, "ctx"),
    )
    return jax.shard_map(
        body,
        mesh=mesh,
        in_specs=placed,
        out_specs=(
            P("exp", "ctx"),
            P("exp", "ctx"),
            P("exp", None),
            P("exp", None),
            P("exp", "ctx"),
            P("exp", "ctx"),
        ),
        check_vma=False,
    )
```

```python
import functools
import math

import jax
import jax.numpy as jnp
from jax import lax
from jax.experimental import pallas as pl
from jax.experimental.pallas import tpu as pltpu
from jax.sharding import PartitionSpec as P

HEAD_SIZE = 128
LANES = 128
ROW_TILE = 16
PAIRS = 4
CHUNK = 512
SMALL_VMEM = 16 * 1024 * 1024
LARGE_VMEM = 20 * 1024 * 1024
EXPERT_VMEM = 16 * 1024 * 1024
BF16 = jnp.bfloat16
F32 = jnp.float32


def dot(a, b, a_dim=1, b_dim=0):
    return lax.dot_general(a, b, (((a_dim,), (b_dim,)), ((), ())), preferred_element_type=F32)


def iota(shape, dim):
    return lax.broadcasted_iota(jnp.int32, shape, dim)


def params(vmem_bytes):
    return pltpu.CompilerParams(vmem_limit_bytes=vmem_bytes, dimension_semantics=("arbitrary",))


def in_hbm(value):
    return pltpu.with_memory_space_constraint(value, pltpu.HBM)


def cost(flops, bytes_accessed, transcendentals=0):
    return pl.CostEstimate(
        flops=int(flops), bytes_accessed=int(bytes_accessed), transcendentals=int(transcendentals)
    )


def power_of_two(value):
    return value > 0 and value & (value - 1) == 0


class Slots:
    def __init__(self, slot_count, width, exp_count, local_experts):
        whole = slot_count // ROW_TILE * ROW_TILE
        rem = slot_count - whole
        blocks = width // LANES
        self.fold = (
            whole > 0
            and rem > 0
            and power_of_two(rem)
            and power_of_two(exp_count)
            and rem * blocks <= whole
            and (rem * exp_count) % ROW_TILE == 0
        )
        self.rows = whole if self.fold or rem == 0 else whole + ROW_TILE
        self.rem = rem if self.fold else 0
        self.blocks = blocks
        self.width = width
        self.columns = width + (LANES if self.fold else 0)
        self.exp_count = exp_count
        self.local = local_experts
        self.experts = exp_count * local_experts
        self.total = self.experts * self.rows
        self.per_expert = exp_count * (self.rows + self.rem)


def route_places(ids, slots):
    top, tokens = ids.shape
    expert = iota((-(-slots.experts // ROW_TILE) * ROW_TILE, tokens), 0)
    hits = [(ids[r : r + 1, :] == expert).astype(F32) for r in range(top)]
    earlier = (iota((tokens, tokens), 0) < iota((tokens, tokens), 1)).astype(BF16)
    before = dot(sum(hits).astype(BF16), earlier)
    found = []
    for r in range(top):
        rank = jnp.sum(hits[r] * before, axis=0, keepdims=True)
        base = ids[r : r + 1, :].astype(F32) * slots.rows
        inside = rank < slots.rows
        main = jnp.where(inside, base + rank, -1.0)
        folded = jnp.where(inside, -65536.0, base + rank - slots.rows)
        found.append((main, folded))
    return found


def as_column(row):
    tokens = row.shape[1]
    return jnp.transpose(jnp.broadcast_to(row, (LANES, tokens)))[:, 0:1]


def dispatch_kernel(slots, weighted, ids_ref, gain_ref, rows_ref, out_ref):
    top, tokens = ids_ref.shape
    places = route_places(ids_ref[...], slots)
    gains = [gain_ref[r : r + 1, :] for r in range(top)]
    slot = iota((slots.total, tokens), 0).astype(F32)
    rows = rows_ref[...]

    def picks(wanted):
        pick = jnp.zeros((slots.total, tokens), F32)
        gain = pick
        for r in range(top):
            here = slot == wanted[r]
            pick = jnp.where(here, 1.0, pick)
            gain = jnp.where(here, gains[r], gain)
        return pick.astype(BF16), gain

    pick, gain = picks([main for main, _ in places])
    taken = dot(pick, rows)
    if weighted:
        taken = taken * jnp.sum(gain, axis=1, keepdims=True)
    out_ref[:, : slots.width] = taken.astype(BF16)
    if slots.fold:
        taken = jnp.zeros((slots.total, LANES), F32)
        total_gain = jnp.zeros((slots.total, tokens), F32)
        for f in range(slots.blocks):
            pick, gain = picks([start + float(f * slots.rem) for _, start in places])
            taken = taken + dot(pick, rows[:, f * LANES : (f + 1) * LANES])
            total_gain = total_gain + gain
        if weighted:
            taken = taken * jnp.sum(total_gain, axis=1, keepdims=True)
        out_ref[:, slots.width :] = taken.astype(BF16)


def dispatch(slots, weighted, ids, gains, rows):
    return pl.pallas_call(
        functools.partial(dispatch_kernel, slots, weighted),
        out_shape=jax.ShapeDtypeStruct((slots.total, slots.columns), BF16),
        compiler_params=pltpu.CompilerParams(vmem_limit_bytes=LARGE_VMEM),
        cost_estimate=cost(4 * slots.total * LANES * slots.width, 4 * slots.total * slots.columns),
        name="dispatch_scaled" if weighted else "dispatch_rows",
    )(in_hbm(ids), in_hbm(gains), in_hbm(rows))


def combine_kernel(slots, weighted, ids_ref, gain_ref, back_ref, out_ref):
    top, tokens = ids_ref.shape
    places = [
        (as_column(main), as_column(start))
        for main, start in route_places(ids_ref[...], slots)
    ]
    gains = [as_column(gain_ref[r : r + 1, :]) if weighted else 1.0 for r in range(top)]
    slot = iota((tokens, slots.total), 1).astype(F32)

    def table(wanted):
        found = jnp.zeros((tokens, slots.total), F32)
        for r in range(top):
            found = jnp.where(slot == wanted[r], gains[r], found)
        return found

    def apply(found, rows):
        high = found.astype(BF16)
        result = dot(high, rows)
        if weighted:
            result = result + dot((found - high.astype(F32)).astype(BF16), rows)
        return result

    result = apply(table([main for main, _ in places]), back_ref[:, : slots.width])
    if slots.fold:
        folded = back_ref[:, slots.width :]
        extra = [
            apply(table([start + float(f * slots.rem) for _, start in places]), folded)
            for f in range(slots.blocks)
        ]
        result = result + jnp.concatenate(extra, axis=1)
    out_ref[...] = result.astype(BF16)


def combine(slots, weighted, ids, gains, back):
    tokens = ids.shape[1]
    return pl.pallas_call(
        functools.partial(combine_kernel, slots, weighted),
        out_shape=jax.ShapeDtypeStruct((tokens, slots.width), BF16),
        compiler_params=pltpu.CompilerParams(vmem_limit_bytes=SMALL_VMEM),
        cost_estimate=cost(8 * slots.total * LANES * slots.width, 4 * slots.total * slots.columns),
        name="combine_out" if weighted else "combine_in",
    )(ids, gains, back)


def fold_table(slots, shape, folded_dim):
    folded = iota(shape, folded_dim)
    plain = iota(shape, 1 - folded_dim)
    rem_bits = int(math.log2(slots.rem))
    exp_bits = int(math.log2(slots.exp_count))
    j = plain & (slots.rem - 1)
    source = (plain >> rem_bits) & (slots.exp_count - 1)
    f = plain >> (rem_bits + exp_bits)
    return (folded == source * slots.rows + f * slots.rem + j).astype(F32).astype(BF16)


def unpack_rows(slots, block):
    flat = block.reshape(slots.exp_count * slots.rows, slots.columns)
    if not slots.fold:
        return flat
    each = slots.exp_count * slots.rem
    plain = dot(
        fold_table(slots, (slots.blocks * each, slots.exp_count * slots.rows), 1),
        flat[:, slots.width :],
    ).astype(BF16)
    extra = jnp.concatenate(
        [plain[f * each : (f + 1) * each] for f in range(slots.blocks)], axis=1
    )
    return jnp.concatenate([flat[:, : slots.width], extra], axis=0)


def pack_rows(slots, rows, out_ref):
    count = slots.exp_count * slots.rows
    main = rows[:count].reshape(slots.exp_count, slots.rows, slots.width)
    out_ref[:, :, : slots.width] = main
    if slots.fold:
        each = slots.exp_count * slots.rem
        stacked = jnp.concatenate(
            [rows[count:, f * LANES : (f + 1) * LANES] for f in range(slots.blocks)], axis=0
        )
        folded = dot(fold_table(slots, (count, slots.blocks * each), 0), stacked).astype(BF16)
        out_ref[:, :, slots.width :] = folded.reshape(slots.exp_count, slots.rows, LANES)


def fetch(sources, targets, sems):
    copies = [
        pltpu.make_async_copy(source, target, sems.at[i])
        for i, (source, target) in enumerate(zip(sources, targets))
    ]
    for copy in copies:
        copy.start()
    return copies


def hold_kernel(expert_ref, gate_ref, up_ref, out_ref, sems):
    e = expert_ref[0]
    for copy in fetch([gate_ref.at[e], up_ref.at[e]], [out_ref.at[0], out_ref.at[1]], sems):
        copy.wait()


def hold(expert, gate_proj, up_proj):
    return expert_call(
        hold_kernel, "hold_weights", pltpu.VMEM((2, *gate_proj.shape[1:]), BF16), expert,
        in_hbm(gate_proj), in_hbm(up_proj), anywhere=(0, 1), copies=2,
    )


def expert_call(kernel, name, out_shape, scalars, *operands, anywhere=(), copies=0, held=None):
    in_vmem = pl.BlockSpec(memory_space=pltpu.VMEM)
    specs = [
        pl.BlockSpec(memory_space=pl.ANY) if i in anywhere else in_vmem
        for i in range(len(operands))
    ]
    if scalars is not None:
        specs = [pl.BlockSpec(memory_space=pltpu.SMEM)] + specs
        operands = (scalars, *operands)
    scratch = [] if held is None else [pltpu.VMEM(held, BF16)]
    if copies:
        scratch.append(pltpu.SemaphoreType.DMA((copies,)))
    return pl.pallas_call(
        kernel,
        in_specs=specs,
        out_specs=[in_vmem] * len(out_shape) if isinstance(out_shape, list) else in_vmem,
        out_shape=out_shape,
        scratch_shapes=scratch,
        compiler_params=pltpu.CompilerParams(vmem_limit_bytes=EXPERT_VMEM),
        name=name,
    )(*operands)


def gate_up_send_kernel(
    slots, order_ref, recv_ref, held_ref, gate_ref, up_ref, out_ref, next_ref, rows_ref, all_ref, sems
):
    e, following = order_ref[0], order_ref[1]
    copies = fetch(
        [recv_ref, gate_ref.at[following], up_ref.at[following]],
        [all_ref, next_ref.at[0], next_ref.at[1]],
        sems,
    )
    copies[0].wait()
    rows = unpack_rows(slots, all_ref[:, e])
    out_ref[0] = dot(rows, held_ref[0]).astype(BF16)
    out_ref[1] = dot(rows, held_ref[1]).astype(BF16)
    rows_ref[...] = unpack_rows(slots, all_ref[:, following])
    for copy in copies[1:]:
        copy.wait()


def gate_up_send(slots, order, recv, held, gate_proj, up_proj):
    out = [
        jax.ShapeDtypeStruct((2, slots.per_expert, gate_proj.shape[2]), BF16),
        pltpu.VMEM(held.shape, BF16),
        jax.ShapeDtypeStruct((slots.per_expert, slots.width), BF16),
    ]
    return expert_call(
        functools.partial(gate_up_send_kernel, slots), "gate_up_send", out, order,
        in_hbm(recv), held, in_hbm(gate_proj), in_hbm(up_proj),
        anywhere=(0, 2, 3), copies=3, held=recv.shape,
    )


def gate_up_keep_kernel(rows_ref, held_ref, arrived_ref, out_ref):
    for i in range(2):
        part = dot(rows_ref[...], held_ref[i]) + arrived_ref[i].astype(F32)
        out_ref[i] = part.astype(BF16)


def gate_up_keep(rows, held, arrived):
    out = jax.ShapeDtypeStruct(arrived.shape, BF16)
    return expert_call(gate_up_keep_kernel, "gate_up_keep", out, None, rows, held, arrived)


def hidden_grad_send_kernel(slots, order_ref, recv_ref, down_ref, out_ref, rows_ref):
    rows = unpack_rows(slots, recv_ref[:, order_ref[0]])
    out_ref[...] = dot(rows, down_ref[order_ref[0]], 1, 1).astype(BF16)
    rows_ref[...] = unpack_rows(slots, recv_ref[:, order_ref[1]])


def hidden_grad_send(slots, order, recv, down_proj):
    out = [
        jax.ShapeDtypeStruct((slots.per_expert, down_proj.shape[1]), BF16),
        jax.ShapeDtypeStruct((slots.per_expert, slots.width), BF16),
    ]
    kernel = functools.partial(hidden_grad_send_kernel, slots)
    return expert_call(kernel, "hidden_grad_send", out, order, recv, down_proj)


def hidden_grad_keep_kernel(expert_ref, rows_ref, down_ref, arrived_ref, out_ref):
    part = dot(rows_ref[...], down_ref[expert_ref[0]], 1, 1) + arrived_ref[...].astype(F32)
    out_ref[...] = part.astype(BF16)


def hidden_grad_keep(expert, rows, down_proj, arrived):
    out = jax.ShapeDtypeStruct(arrived.shape, BF16)
    return expert_call(
        hidden_grad_keep_kernel, "hidden_grad_keep", out, expert, rows, down_proj, arrived
    )


def store_rows(slots, rows, expert, packed_ref, out_ref, sem):
    pack_rows(slots, rows, packed_ref)
    copy = pltpu.make_async_copy(packed_ref, out_ref.at[:, expert], sem)
    copy.start()
    return copy


def packed_shape(slots):
    return (slots.exp_count, slots.local, slots.rows, slots.columns)


def packed_scratch(slots):
    return pltpu.VMEM((slots.local, slots.exp_count, slots.rows, slots.columns), BF16)


def route_out_kernel(slots, order_ref, mine_ref, other_ref, down_ref, out_ref, packed_ref, sems):
    stores = []
    for at, hidden_ref in enumerate((mine_ref, other_ref)):
        e = order_ref[at]
        rows = dot(hidden_ref[...], down_ref[e]).astype(BF16)
        stores.append(store_rows(slots, rows, e, packed_ref.at[at], out_ref, sems.at[at]))
    for store in stores:
        store.wait()


def route_out(slots, order, mine, other, down_proj):
    in_vmem = pl.BlockSpec(memory_space=pltpu.VMEM)
    return pl.pallas_call(
        functools.partial(route_out_kernel, slots),
        in_specs=[pl.BlockSpec(memory_space=pltpu.SMEM), in_vmem, in_vmem, in_vmem],
        out_specs=pl.BlockSpec(memory_space=pltpu.HBM),
        out_shape=pltpu.HBM(packed_shape(slots), BF16),
        scratch_shapes=[packed_scratch(slots), pltpu.SemaphoreType.DMA((slots.local,))],
        compiler_params=pltpu.CompilerParams(vmem_limit_bytes=EXPERT_VMEM),
        name="route_out",
    )(order, mine, other, down_proj)


def route_in_kernel(
    slots, order_ref, mine_ref, other_ref, held_ref, gate_ref, up_ref, out_ref,
    mine_held, other_held, next_ref, packed_ref, sems, out_sems,
):
    first, second = order_ref[0], order_ref[1]
    copies = fetch(
        [mine_ref, gate_ref.at[second], up_ref.at[second], other_ref],
        [mine_held, next_ref.at[0], next_ref.at[1], other_held],
        sems,
    )
    copies[0].wait()
    total = dot(mine_held[0], held_ref[0], 1, 1) + dot(mine_held[1], held_ref[1], 1, 1)
    rows = total.astype(BF16)
    stores = [store_rows(slots, rows, first, packed_ref.at[0], out_ref, out_sems.at[0])]
    for copy in copies[1:]:
        copy.wait()
    total = dot(other_held[0], next_ref[0], 1, 1) + dot(other_held[1], next_ref[1], 1, 1)
    rows = total.astype(BF16)
    stores.append(store_rows(slots, rows, second, packed_ref.at[1], out_ref, out_sems.at[1]))
    for store in stores:
        store.wait()


def route_in(slots, order, mine, other, held, gate_proj, up_proj):
    anywhere = pl.BlockSpec(memory_space=pl.ANY)
    return pl.pallas_call(
        functools.partial(route_in_kernel, slots),
        in_specs=[
            pl.BlockSpec(memory_space=pltpu.SMEM), anywhere, anywhere,
            pl.BlockSpec(memory_space=pltpu.VMEM), anywhere, anywhere,
        ],
        out_specs=pl.BlockSpec(memory_space=pltpu.HBM),
        out_shape=pltpu.HBM(packed_shape(slots), BF16),
        scratch_shapes=[
            pltpu.VMEM(mine.shape, BF16),
            pltpu.VMEM(other.shape, BF16),
            pltpu.VMEM(held.shape, BF16),
            packed_scratch(slots),
            pltpu.SemaphoreType.DMA((4,)),
            pltpu.SemaphoreType.DMA((slots.local,)),
        ],
        compiler_params=pltpu.CompilerParams(vmem_limit_bytes=EXPERT_VMEM),
        name="route_in",
    )(order, mine, other, held, in_hbm(gate_proj), in_hbm(up_proj))


def attention_kernel(offsets, tokens, chunk, first, last, me_ref, q_ref, g_ref, kv_ref, kv_far_ref, *refs):
    if not first:
        carry_ref, refs = refs[0], refs[3:]
    out_ref, qgrad_ref = refs[:2]
    if last:
        keep_ref, send_ref = refs[2:4]
    else:
        carried_ref = refs[2]
    scores_ref, low_ref, key_t, value_t, key_acc, value_acc = refs[-6:]
    d = HEAD_SIZE
    step = pl.program_id(0)
    me = me_ref[0]
    half = kv_ref.shape[0]
    seq = 2 * half
    scale = d ** (-0.5)
    to_base2 = scale * math.log2(math.e)

    @pl.when(step == 0)
    def _():
        for start, ref in ((0, kv_ref), (half, kv_far_ref)):
            for at in range(0, half, tokens):
                both = jnp.transpose(ref[at : at + tokens, :])
                key_t[:, start + at : start + at + tokens] = both[:d]
                value_t[:, start + at : start + at + tokens] = both[d:]
        if first:
            key_acc[...] = jnp.zeros_like(key_acc)
            value_acc[...] = jnp.zeros_like(value_acc)
        else:
            key_acc[...] = carry_ref[:, :d]
            value_acc[...] = carry_ref[:, d:]

    def piece(at, column):
        ref, start = (kv_ref, at) if at < half else (kv_far_ref, at - half)
        return ref[start : start + chunk, column : column + d]

    pairs = scores_ref.shape[0]
    lanes = scores_ref.shape[2]
    heads = lanes // tokens
    chunks = range(0, seq, chunk)
    ahead = iota((tokens, lanes), 0) - (iota((tokens, lanes), 1) & (tokens - 1))
    limits = [(me - (me ^ offset)) * tokens for offset in offsets]

    def columns(pair, h):
        start = (pair * heads + h) * d
        return slice(start, start + d)

    def stacked(ref, pair):
        return jnp.concatenate([ref[:, columns(pair, h)] for h in range(heads)], axis=0)

    every = range(pairs)
    q = [stacked(q_ref, pair) for pair in every]
    g = [stacked(g_ref, pair) for pair in every]
    q_t = [jnp.transpose(value) for value in q]
    g_t = [jnp.transpose(value) for value in g]
    top, inverse, row_dot = {}, {}, {}

    def keep_rows(ref, pair, value):
        low = value.astype(BF16)
        for h in range(heads):
            ref[:, columns(pair, h)] = jnp.transpose(low[:, h * tokens : (h + 1) * tokens])

    def score_stage(pair):
        largest = jnp.full((1, lanes), -jnp.inf, F32)
        for at in chunks:
            scores = dot(piece(at, 0), q_t[pair])
            for part in range(0, chunk, tokens):
                allowed = ahead <= limits[(at + part) // tokens]
                some = jnp.where(allowed, scores[part : part + tokens], -jnp.inf)
                scores_ref[pair, at + part : at + part + tokens, :] = some
                largest = jnp.maximum(largest, jnp.max(some, axis=0, keepdims=True))
            yield
        top[pair] = largest * to_base2

    def raise_stage(pair):
        total = jnp.zeros((1, lanes), F32)
        for at in chunks:
            raised = jnp.exp2(scores_ref[pair, at : at + chunk, :] * to_base2 - top[pair])
            scores_ref[pair, at : at + chunk, :] = raised
            total = total + jnp.sum(raised, axis=0, keepdims=True)
            yield
        inverse[pair] = 1.0 / total

    def attend_stage(pair):
        attended = jnp.zeros((d, lanes), F32)
        for at in chunks:
            low = (scores_ref[pair, at : at + chunk, :] * inverse[pair]).astype(BF16)
            low_ref[pair, at : at + chunk, :] = low
            attended = attended + dot(value_t[:, at : at + chunk], low)
            value_acc[at : at + chunk, :] += dot(low, g[pair])
            yield
        keep_rows(out_ref, pair, attended)
        attended = attended.astype(BF16).astype(F32)
        row_dot[pair] = jnp.sum(g_t[pair].astype(F32) * attended, axis=0, keepdims=True)

    def back_stage(pair):
        query_back = jnp.zeros((d, lanes), F32)
        for at in chunks:
            low = low_ref[pair, at : at + chunk, :]
            prob_grad = dot(piece(at, d), g_t[pair])
            score_grad = (low.astype(F32) * (prob_grad - row_dot[pair])).astype(BF16)
            query_back = query_back + dot(key_t[:, at : at + chunk], score_grad)
            key_acc[at : at + chunk, :] += dot(score_grad, q[pair])
            yield
        keep_rows(qgrad_ref, pair, query_back * scale)

    stages = (score_stage, raise_stage, attend_stage, back_stage)
    for slot in range(pairs + len(stages) - 1):
        running = [stages[slot - pair](pair) for pair in every if 0 <= slot - pair < len(stages)]
        while running:
            running = [stage for stage in running if next(stage, True) is None]

    @pl.when(step == pl.num_programs(0) - 1)
    def _():
        if last:
            keep_ref[:, :d] = key_acc[:half, :] * scale
            keep_ref[:, d:] = value_acc[:half, :]
            send_ref[:, :d] = (key_acc[half:, :] * scale).astype(BF16)
            send_ref[:, d:] = value_acc[half:, :].astype(BF16)
        else:
            carried_ref[:, :d] = key_acc[...]
            carried_ref[:, d:] = value_acc[...]


def attention(me, offsets, queries, attn_grad, kv_near, kv_far, part, parts, carried=None):
    tokens, columns = queries.shape
    half, both = kv_near.shape
    seq = 2 * half
    heads = columns // HEAD_SIZE
    group = 4 if heads % (4 * parts) == 0 and seq <= 2048 else 2 if heads % (2 * parts) == 0 else 1
    pairs = PAIRS if heads % (group * PAIRS * parts) == 0 and seq <= 2048 else 1
    lanes = group * tokens
    chunk = min(CHUNK, half)
    steps = heads // (group * pairs * parts)
    first, last = part == 0, part == parts - 1
    tile = pl.BlockSpec((tokens, pairs * group * HEAD_SIZE), lambda i, m: (0, i + part * steps))
    whole = pl.BlockSpec((half, both), lambda i, m: (0, 0))
    sums = pl.BlockSpec((seq, both), lambda i, m: (0, 0))
    held = pl.BlockSpec(memory_space=pl.ANY)
    wide = jax.ShapeDtypeStruct(queries.shape, BF16)
    if last:
        final = [jax.ShapeDtypeStruct((half, both), F32), jax.ShapeDtypeStruct((half, both), BF16)]
    else:
        final = [jax.ShapeDtypeStruct((seq, both), F32)]
    return pl.pallas_call(
        functools.partial(attention_kernel, offsets, tokens, chunk, first, last),
        grid_spec=pltpu.PrefetchScalarGridSpec(
            num_scalar_prefetch=1,
            grid=(steps,),
            in_specs=[tile, tile, whole, whole] + ([] if first else [sums, held, held]),
            out_specs=[tile, tile] + ([whole, whole] if last else [sums]),
            scratch_shapes=[
                pltpu.VMEM((pairs, seq, lanes), F32),
                pltpu.VMEM((pairs, seq, lanes), BF16),
                pltpu.VMEM((HEAD_SIZE, seq), BF16),
                pltpu.VMEM((HEAD_SIZE, seq), BF16),
                pltpu.VMEM((seq, HEAD_SIZE), F32),
                pltpu.VMEM((seq, HEAD_SIZE), F32),
            ],
        ),
        out_shape=[wide, wide] + final,
        input_output_aliases={} if first else {6: 0, 7: 1},
        compiler_params=params(LARGE_VMEM),
        cost_estimate=cost(
            12 * tokens * columns * seq // parts,
            8 * tokens * columns // parts,
            tokens * heads * seq // parts,
        ),
        name="attention",
    )(me, in_hbm(queries), in_hbm(attn_grad), in_hbm(kv_near), in_hbm(kv_far), *(() if first else (carried[2], carried[0], carried[1])))


def swap(value, axis, bit):
    count = lax.axis_size(axis)
    return lax.ppermute(value, axis, [(i, i ^ bit) for i in range(count)])


def after(value, *earlier):
    return lax.optimization_barrier((value, *earlier))[0]


def far_bits(count):
    bits = []
    bit = count // 2
    while bit >= 1:
        bits.append(bit)
        bit //= 2
    return bits


def spread_sum(part, ctx_count, beside):
    result = None
    bit = 2
    while True:
        arrived = swap(part.astype(BF16), "ctx", bit)
        if result is None:
            result = beside(part)
            arrived = after(arrived, *result)
        bit *= 2
        if bit >= ctx_count:
            return (part, arrived), result
        part = part.astype(F32) + arrived.astype(F32)


def total_of(addends):
    return addends[0].astype(F32) + addends[1].astype(F32)


def activate(gate, up):
    return (jax.nn.silu(gate) * up).astype(BF16)


def gate_backward(hidden_grad, gate, up):
    s = jax.nn.sigmoid(gate)
    gate_back = (hidden_grad * up * s * (1.0 + gate * (1.0 - s))).astype(BF16)
    up_back = (hidden_grad * (gate * s)).astype(BF16)
    return jnp.stack([gate_back, up_back])


def body(
    queries, key_proj, value_matrix_rows, attn_grad, moe_input, moe_grad,
    expert_ids, route_weights, gate_proj, up_proj, down_proj,
):
    ctx_count = lax.axis_size("ctx")
    exp_count = lax.axis_size("exp")
    ctx_index = lax.axis_index("ctx")
    exp_index = lax.axis_index("exp")
    tokens = queries.shape[0]
    d = HEAD_SIZE
    kv_heads = key_proj.shape[1] // d
    sharers = ctx_count // kv_heads
    kv_head = ctx_index // sharers
    width = moe_input.shape[1]
    local = gate_proj.shape[0]
    expert_total = local * exp_count
    slot_count = 2 * ((tokens + expert_total - 2) // (expert_total - 1))
    slots = Slots(slot_count, width, exp_count, local)
    core = ctx_index % 2
    mine = core.astype(jnp.int32).reshape(1)
    other = 1 - mine
    order = jnp.concatenate([mine, other])
    shape = (exp_count, local, slots.rows, slots.columns)

    def exchange(rows):
        flat = rows.reshape(exp_count, local * slots.rows, slots.columns)
        return lax.all_to_all(flat, "exp", split_axis=0, concat_axis=0, tiled=True)

    me = exp_index.astype(jnp.int32).reshape(1)
    ids = expert_ids.T
    gains = route_weights.T

    kv = jnp.concatenate(
        [
            lax.dynamic_slice_in_dim(key_proj, kv_head * d, d, 1),
            lax.dynamic_slice_in_dim(value_matrix_rows, kv_head * d, d, 1),
        ],
        axis=1,
    )
    send_rows = dispatch(slots, False, ids, gains, moe_input)
    offsets = [0]
    kv_far = None
    for bit in far_bits(exp_count):
        if kv_far is not None:
            kv = jnp.concatenate([kv, after(kv_far, send_rows)], axis=0)
        if bit == 2:
            recv_rows = exchange(after(send_rows, kv)).reshape(shape)
        kv_far = swap(kv, "exp", bit)
        offsets = offsets + [o ^ bit for o in offsets]
    send_scaled = dispatch(slots, True, ids, gains, after(moe_grad, send_rows))
    held = hold(other, after(gate_proj, send_scaled), up_proj)

    def heads(part, carried, earlier):
        return attention(
            me, tuple(offsets), after(queries, earlier), attn_grad, kv, kv_far, part, 1, carried
        )

    recv_rows = after(recv_rows, kv)
    gu_send, held, rows = gate_up_send(slots, order[::-1], recv_rows, held, gate_proj, up_proj)
    gu_recv = swap(gu_send, "ctx", 1)
    gu_part = gate_up_keep(rows, held, gu_recv)
    recv_scaled = exchange(after(send_scaled, gu_part)).reshape(shape)
    gate_up_sum, (attn_out, query_grad, kv_keep, kv_send) = spread_sum(
        gu_part, ctx_count, lambda part: heads(0, None, part)
    )
    kv_recv = swap(kv_send, "exp", 1)
    hidden = activate(*total_of(gate_up_sum))
    hidden_other = swap(hidden, "ctx", 1)
    hg_send, rows = hidden_grad_send(slots, order[::-1], after(recv_scaled, hidden), down_proj)
    hg_recv = swap(hg_send, "ctx", 1)
    out_rows = route_out(slots, order, after(hidden, hg_send), hidden_other, down_proj)
    back_out = exchange(after(out_rows, kv_recv)).reshape(slots.total, slots.columns)

    hg_part = hidden_grad_keep(mine, after(rows, out_rows), down_proj, hg_recv)
    kv_sum = kv_keep + after(kv_recv, hg_part).astype(F32)
    kv_low = kv_sum.astype(BF16)
    blocks = exp_count // 2
    kv_parts = [
        swap(kv_low[i * tokens : (i + 1) * tokens], "exp", offsets[i]) for i in range(1, blocks)
    ]
    gate_up_sum = [after(value, hg_part) for value in gate_up_sum]
    gate_up_total = total_of(gate_up_sum)
    held = hold(mine, after(gate_proj, hg_part), up_proj)
    hg_sum, _ = spread_sum(hg_part, ctx_count, lambda part: (kv_low, gate_up_total, held))
    back = gate_backward(total_of(hg_sum), *gate_up_total)
    back_other = swap(back, "ctx", 1)
    in_rows = route_in(slots, order, back, back_other, held, gate_proj, up_proj)
    kv_total = kv_sum[:tokens]
    for part in kv_parts:
        kv_total = kv_total + after(part, in_rows).astype(F32)
    kv_total = kv_total.astype(BF16)
    back_in = exchange(after(in_rows, kv_total)).reshape(slots.total, slots.columns)

    moe_out = combine(slots, True, ids, gains, after(back_out, in_rows))
    input_grad = combine(slots, False, ids, gains, back_in)

    kv_every = lax.all_gather(after(kv_total, in_rows), "ctx", axis=0, tiled=False)
    if sharers > 1:
        kv_every = kv_every.astype(F32).reshape(kv_heads, sharers, tokens, 2 * d).sum(axis=1)
    kv_every = kv_every.astype(BF16)
    key_grad = jnp.concatenate([kv_every[h, :, :d] for h in range(kv_heads)], axis=1)
    value_grad = jnp.concatenate([kv_every[h, :, d:] for h in range(kv_heads)], axis=1)
    return (attn_out, query_grad, key_grad, value_grad, moe_out, input_grad)


def solution(mesh):
    placed = (
        P("exp", "ctx"),
        P("exp", None),
        P("exp", None),
        P("exp", "ctx"),
        P("exp", "ctx"),
        P("exp", "ctx"),
        P("exp", None),
        P("exp", None),
        P("exp", "ctx", None),
        P("exp", "ctx", None),
        P("exp", None, "ctx"),
    )
    return jax.shard_map(
        body,
        mesh=mesh,
        in_specs=placed,
        out_specs=(
            P("exp", "ctx"),
            P("exp", "ctx"),
            P("exp", None),
            P("exp", None),
            P("exp", "ctx"),
            P("exp", "ctx"),
        ),
        check_vma=False,
    )
```

```python
import functools
import math

import jax
import jax.numpy as jnp
from jax import lax
from jax.experimental import pallas as pl
from jax.experimental.pallas import tpu as pltpu
from jax.sharding import PartitionSpec as P

HEAD_SIZE = 128
LANES = 128
ROW_TILE = 16
PAIRS = 4
CHUNK = 512
SMALL_VMEM = 16 * 1024 * 1024
LARGE_VMEM = 20 * 1024 * 1024
EXPERT_VMEM = 16 * 1024 * 1024
BF16 = jnp.bfloat16
F32 = jnp.float32


def dot(a, b, a_dim=1, b_dim=0):
    return lax.dot_general(a, b, (((a_dim,), (b_dim,)), ((), ())), preferred_element_type=F32)


def iota(shape, dim):
    return lax.broadcasted_iota(jnp.int32, shape, dim)


def params(vmem_bytes):
    return pltpu.CompilerParams(vmem_limit_bytes=vmem_bytes, dimension_semantics=("arbitrary",))


def in_hbm(value):
    return pltpu.with_memory_space_constraint(value, pltpu.HBM)


def cost(flops, bytes_accessed, transcendentals=0):
    return pl.CostEstimate(
        flops=int(flops), bytes_accessed=int(bytes_accessed), transcendentals=int(transcendentals)
    )


def power_of_two(value):
    return value > 0 and value & (value - 1) == 0


class Slots:
    def __init__(self, slot_count, width, exp_count, local_experts):
        whole = slot_count // ROW_TILE * ROW_TILE
        rem = slot_count - whole
        blocks = width // LANES
        self.fold = (
            whole > 0
            and rem > 0
            and power_of_two(rem)
            and power_of_two(exp_count)
            and rem * blocks <= whole
            and (rem * exp_count) % ROW_TILE == 0
        )
        self.rows = whole if self.fold or rem == 0 else whole + ROW_TILE
        self.rem = rem if self.fold else 0
        self.blocks = blocks
        self.width = width
        self.columns = width + (LANES if self.fold else 0)
        self.exp_count = exp_count
        self.local = local_experts
        self.experts = exp_count * local_experts
        self.total = self.experts * self.rows
        self.per_expert = exp_count * (self.rows + self.rem)


def route_places(ids, slots):
    top, tokens = ids.shape
    expert = iota((-(-slots.experts // ROW_TILE) * ROW_TILE, tokens), 0)
    hits = [(ids[r : r + 1, :] == expert).astype(F32) for r in range(top)]
    earlier = (iota((tokens, tokens), 0) < iota((tokens, tokens), 1)).astype(BF16)
    before = dot(sum(hits).astype(BF16), earlier)
    found = []
    for r in range(top):
        rank = jnp.sum(hits[r] * before, axis=0, keepdims=True)
        base = ids[r : r + 1, :].astype(F32) * slots.rows
        inside = rank < slots.rows
        main = jnp.where(inside, base + rank, -1.0)
        folded = jnp.where(inside, -65536.0, base + rank - slots.rows)
        found.append((main, folded))
    return found


def as_column(row):
    tokens = row.shape[1]
    return jnp.transpose(jnp.broadcast_to(row, (LANES, tokens)))[:, 0:1]


def dispatch_kernel(slots, weighted, ids_ref, gain_ref, rows_ref, out_ref):
    top, tokens = ids_ref.shape
    places = route_places(ids_ref[...], slots)
    gains = [gain_ref[r : r + 1, :] for r in range(top)]
    slot = iota((slots.total, tokens), 0).astype(F32)
    rows = rows_ref[...]

    def picks(wanted):
        pick = jnp.zeros((slots.total, tokens), F32)
        gain = pick
        for r in range(top):
            here = slot == wanted[r]
            pick = jnp.where(here, 1.0, pick)
            gain = jnp.where(here, gains[r], gain)
        return pick.astype(BF16), gain

    pick, gain = picks([main for main, _ in places])
    taken = dot(pick, rows)
    if weighted:
        taken = taken * jnp.sum(gain, axis=1, keepdims=True)
    out_ref[:, : slots.width] = taken.astype(BF16)
    if slots.fold:
        taken = jnp.zeros((slots.total, LANES), F32)
        total_gain = jnp.zeros((slots.total, tokens), F32)
        for f in range(slots.blocks):
            pick, gain = picks([start + float(f * slots.rem) for _, start in places])
            taken = taken + dot(pick, rows[:, f * LANES : (f + 1) * LANES])
            total_gain = total_gain + gain
        if weighted:
            taken = taken * jnp.sum(total_gain, axis=1, keepdims=True)
        out_ref[:, slots.width :] = taken.astype(BF16)


def dispatch(slots, weighted, ids, gains, rows):
    return pl.pallas_call(
        functools.partial(dispatch_kernel, slots, weighted),
        out_shape=jax.ShapeDtypeStruct((slots.total, slots.columns), BF16),
        compiler_params=pltpu.CompilerParams(vmem_limit_bytes=LARGE_VMEM),
        cost_estimate=cost(4 * slots.total * LANES * slots.width, 4 * slots.total * slots.columns),
        name="dispatch_scaled" if weighted else "dispatch_rows",
    )(in_hbm(ids), in_hbm(gains), in_hbm(rows))


def combine_kernel(slots, weighted, ids_ref, gain_ref, back_ref, out_ref):
    top, tokens = ids_ref.shape
    places = [
        (as_column(main), as_column(start))
        for main, start in route_places(ids_ref[...], slots)
    ]
    gains = [as_column(gain_ref[r : r + 1, :]) if weighted else 1.0 for r in range(top)]
    slot = iota((tokens, slots.total), 1).astype(F32)

    def table(wanted):
        found = jnp.zeros((tokens, slots.total), F32)
        for r in range(top):
            found = jnp.where(slot == wanted[r], gains[r], found)
        return found

    def apply(found, rows):
        high = found.astype(BF16)
        result = dot(high, rows)
        if weighted:
            result = result + dot((found - high.astype(F32)).astype(BF16), rows)
        return result

    result = apply(table([main for main, _ in places]), back_ref[:, : slots.width])
    if slots.fold:
        folded = back_ref[:, slots.width :]
        extra = [
            apply(table([start + float(f * slots.rem) for _, start in places]), folded)
            for f in range(slots.blocks)
        ]
        result = result + jnp.concatenate(extra, axis=1)
    out_ref[...] = result.astype(BF16)


def combine(slots, weighted, ids, gains, back):
    tokens = ids.shape[1]
    return pl.pallas_call(
        functools.partial(combine_kernel, slots, weighted),
        out_shape=jax.ShapeDtypeStruct((tokens, slots.width), BF16),
        compiler_params=pltpu.CompilerParams(vmem_limit_bytes=SMALL_VMEM),
        cost_estimate=cost(8 * slots.total * LANES * slots.width, 4 * slots.total * slots.columns),
        name="combine_out" if weighted else "combine_in",
    )(ids, gains, back)


def fold_table(slots, shape, folded_dim):
    folded = iota(shape, folded_dim)
    plain = iota(shape, 1 - folded_dim)
    rem_bits = int(math.log2(slots.rem))
    exp_bits = int(math.log2(slots.exp_count))
    j = plain & (slots.rem - 1)
    source = (plain >> rem_bits) & (slots.exp_count - 1)
    f = plain >> (rem_bits + exp_bits)
    return (folded == source * slots.rows + f * slots.rem + j).astype(F32).astype(BF16)


def unpack_rows(slots, block):
    flat = block.reshape(slots.exp_count * slots.rows, slots.columns)
    if not slots.fold:
        return flat
    each = slots.exp_count * slots.rem
    plain = dot(
        fold_table(slots, (slots.blocks * each, slots.exp_count * slots.rows), 1),
        flat[:, slots.width :],
    ).astype(BF16)
    extra = jnp.concatenate(
        [plain[f * each : (f + 1) * each] for f in range(slots.blocks)], axis=1
    )
    return jnp.concatenate([flat[:, : slots.width], extra], axis=0)


def pack_rows(slots, rows, out_ref):
    count = slots.exp_count * slots.rows
    main = rows[:count].reshape(slots.exp_count, slots.rows, slots.width)
    out_ref[:, :, : slots.width] = main
    if slots.fold:
        each = slots.exp_count * slots.rem
        stacked = jnp.concatenate(
            [rows[count:, f * LANES : (f + 1) * LANES] for f in range(slots.blocks)], axis=0
        )
        folded = dot(fold_table(slots, (count, slots.blocks * each), 0), stacked).astype(BF16)
        out_ref[:, :, slots.width :] = folded.reshape(slots.exp_count, slots.rows, LANES)


def fetch(sources, targets, sems):
    copies = [
        pltpu.make_async_copy(source, target, sems.at[i])
        for i, (source, target) in enumerate(zip(sources, targets))
    ]
    for copy in copies:
        copy.start()
    return copies


def hold_kernel(expert_ref, gate_ref, up_ref, out_ref, sems):
    e = expert_ref[0]
    for copy in fetch([gate_ref.at[e], up_ref.at[e]], [out_ref.at[0], out_ref.at[1]], sems):
        copy.wait()


def hold(expert, gate_proj, up_proj):
    return expert_call(
        hold_kernel, "hold_weights", pltpu.VMEM((2, *gate_proj.shape[1:]), BF16), expert,
        in_hbm(gate_proj), in_hbm(up_proj), anywhere=(0, 1), copies=2,
    )


def expert_call(kernel, name, out_shape, scalars, *operands, anywhere=(), copies=0, held=None):
    in_vmem = pl.BlockSpec(memory_space=pltpu.VMEM)
    specs = [
        pl.BlockSpec(memory_space=pl.ANY) if i in anywhere else in_vmem
        for i in range(len(operands))
    ]
    if scalars is not None:
        specs = [pl.BlockSpec(memory_space=pltpu.SMEM)] + specs
        operands = (scalars, *operands)
    scratch = [] if held is None else [pltpu.VMEM(held, BF16)]
    if copies:
        scratch.append(pltpu.SemaphoreType.DMA((copies,)))
    return pl.pallas_call(
        kernel,
        in_specs=specs,
        out_specs=[in_vmem] * len(out_shape) if isinstance(out_shape, list) else in_vmem,
        out_shape=out_shape,
        scratch_shapes=scratch,
        compiler_params=pltpu.CompilerParams(vmem_limit_bytes=EXPERT_VMEM),
        name=name,
    )(*operands)


def gate_up_send_kernel(
    slots, order_ref, recv_ref, held_ref, gate_ref, up_ref, out_ref, next_ref, rows_ref, all_ref, sems
):
    e, following = order_ref[0], order_ref[1]
    copies = fetch(
        [recv_ref, gate_ref.at[following], up_ref.at[following]],
        [all_ref, next_ref.at[0], next_ref.at[1]],
        sems,
    )
    copies[0].wait()
    rows = unpack_rows(slots, all_ref[:, e])
    out_ref[0] = dot(rows, held_ref[0]).astype(BF16)
    out_ref[1] = dot(rows, held_ref[1]).astype(BF16)
    rows_ref[...] = unpack_rows(slots, all_ref[:, following])
    for copy in copies[1:]:
        copy.wait()


def gate_up_send(slots, order, recv, held, gate_proj, up_proj):
    out = [
        jax.ShapeDtypeStruct((2, slots.per_expert, gate_proj.shape[2]), BF16),
        pltpu.VMEM(held.shape, BF16),
        jax.ShapeDtypeStruct((slots.per_expert, slots.width), BF16),
    ]
    return expert_call(
        functools.partial(gate_up_send_kernel, slots), "gate_up_send", out, order,
        in_hbm(recv), held, in_hbm(gate_proj), in_hbm(up_proj),
        anywhere=(0, 2, 3), copies=3, held=recv.shape,
    )


def gate_up_keep_kernel(rows_ref, held_ref, arrived_ref, out_ref):
    for i in range(2):
        part = dot(rows_ref[...], held_ref[i]) + arrived_ref[i].astype(F32)
        out_ref[i] = part.astype(BF16)


def gate_up_keep(rows, held, arrived):
    out = jax.ShapeDtypeStruct(arrived.shape, BF16)
    return expert_call(gate_up_keep_kernel, "gate_up_keep", out, None, rows, held, arrived)


def hidden_grad_send_kernel(slots, order_ref, recv_ref, down_ref, out_ref, rows_ref):
    rows = unpack_rows(slots, recv_ref[:, order_ref[0]])
    out_ref[...] = dot(rows, down_ref[order_ref[0]], 1, 1).astype(BF16)
    rows_ref[...] = unpack_rows(slots, recv_ref[:, order_ref[1]])


def hidden_grad_send(slots, order, recv, down_proj):
    out = [
        jax.ShapeDtypeStruct((slots.per_expert, down_proj.shape[1]), BF16),
        jax.ShapeDtypeStruct((slots.per_expert, slots.width), BF16),
    ]
    kernel = functools.partial(hidden_grad_send_kernel, slots)
    return expert_call(kernel, "hidden_grad_send", out, order, recv, down_proj)


def hidden_grad_keep_kernel(expert_ref, rows_ref, down_ref, arrived_ref, out_ref):
    part = dot(rows_ref[...], down_ref[expert_ref[0]], 1, 1) + arrived_ref[...].astype(F32)
    out_ref[...] = part.astype(BF16)


def hidden_grad_keep(expert, rows, down_proj, arrived):
    out = jax.ShapeDtypeStruct(arrived.shape, BF16)
    return expert_call(
        hidden_grad_keep_kernel, "hidden_grad_keep", out, expert, rows, down_proj, arrived
    )


def store_rows(slots, rows, expert, packed_ref, out_ref, sem):
    pack_rows(slots, rows, packed_ref)
    copy = pltpu.make_async_copy(packed_ref, out_ref.at[:, expert], sem)
    copy.start()
    return copy


def packed_shape(slots):
    return (slots.exp_count, slots.local, slots.rows, slots.columns)


def packed_scratch(slots):
    return pltpu.VMEM((slots.local, slots.exp_count, slots.rows, slots.columns), BF16)


def route_out_kernel(slots, order_ref, mine_ref, other_ref, down_ref, out_ref, packed_ref, sems):
    stores = []
    for at, hidden_ref in enumerate((mine_ref, other_ref)):
        e = order_ref[at]
        rows = dot(hidden_ref[...], down_ref[e]).astype(BF16)
        stores.append(store_rows(slots, rows, e, packed_ref.at[at], out_ref, sems.at[at]))
    for store in stores:
        store.wait()


def route_out(slots, order, mine, other, down_proj):
    in_vmem = pl.BlockSpec(memory_space=pltpu.VMEM)
    return pl.pallas_call(
        functools.partial(route_out_kernel, slots),
        in_specs=[pl.BlockSpec(memory_space=pltpu.SMEM), in_vmem, in_vmem, in_vmem],
        out_specs=pl.BlockSpec(memory_space=pltpu.HBM),
        out_shape=pltpu.HBM(packed_shape(slots), BF16),
        scratch_shapes=[packed_scratch(slots), pltpu.SemaphoreType.DMA((slots.local,))],
        compiler_params=pltpu.CompilerParams(vmem_limit_bytes=EXPERT_VMEM),
        name="route_out",
    )(order, mine, other, down_proj)


def route_in_kernel(
    slots, order_ref, mine_ref, other_ref, held_ref, gate_ref, up_ref, out_ref,
    mine_held, other_held, next_ref, packed_ref, sems, out_sems,
):
    first, second = order_ref[0], order_ref[1]
    copies = fetch(
        [mine_ref, gate_ref.at[second], up_ref.at[second], other_ref],
        [mine_held, next_ref.at[0], next_ref.at[1], other_held],
        sems,
    )
    copies[0].wait()
    total = dot(mine_held[0], held_ref[0], 1, 1) + dot(mine_held[1], held_ref[1], 1, 1)
    rows = total.astype(BF16)
    stores = [store_rows(slots, rows, first, packed_ref.at[0], out_ref, out_sems.at[0])]
    for copy in copies[1:]:
        copy.wait()
    total = dot(other_held[0], next_ref[0], 1, 1) + dot(other_held[1], next_ref[1], 1, 1)
    rows = total.astype(BF16)
    stores.append(store_rows(slots, rows, second, packed_ref.at[1], out_ref, out_sems.at[1]))
    for store in stores:
        store.wait()


def route_in(slots, order, mine, other, held, gate_proj, up_proj):
    anywhere = pl.BlockSpec(memory_space=pl.ANY)
    return pl.pallas_call(
        functools.partial(route_in_kernel, slots),
        in_specs=[
            pl.BlockSpec(memory_space=pltpu.SMEM), anywhere, anywhere,
            pl.BlockSpec(memory_space=pltpu.VMEM), anywhere, anywhere,
        ],
        out_specs=pl.BlockSpec(memory_space=pltpu.HBM),
        out_shape=pltpu.HBM(packed_shape(slots), BF16),
        scratch_shapes=[
            pltpu.VMEM(mine.shape, BF16),
            pltpu.VMEM(other.shape, BF16),
            pltpu.VMEM(held.shape, BF16),
            packed_scratch(slots),
            pltpu.SemaphoreType.DMA((4,)),
            pltpu.SemaphoreType.DMA((slots.local,)),
        ],
        compiler_params=pltpu.CompilerParams(vmem_limit_bytes=EXPERT_VMEM),
        name="route_in",
    )(order, mine, other, held, in_hbm(gate_proj), in_hbm(up_proj))


def attention_kernel(offsets, tokens, chunk, first, last, me_ref, q_ref, g_ref, kv_ref, kv_far_ref, *refs):
    if not first:
        carry_ref, refs = refs[0], refs[3:]
    out_ref, qgrad_ref = refs[:2]
    if last:
        keep_ref, send_ref = refs[2:4]
    else:
        carried_ref = refs[2]
    scores_ref, low_ref, key_t, value_t, key_acc, value_acc = refs[-6:]
    d = HEAD_SIZE
    step = pl.program_id(0)
    me = me_ref[0]
    half = kv_ref.shape[0]
    seq = 2 * half
    scale = d ** (-0.5)
    to_base2 = scale * math.log2(math.e)

    @pl.when(step == 0)
    def _():
        for start, ref in ((0, kv_ref), (half, kv_far_ref)):
            for at in range(0, half, tokens):
                both = jnp.transpose(ref[at : at + tokens, :])
                key_t[:, start + at : start + at + tokens] = both[:d]
                value_t[:, start + at : start + at + tokens] = both[d:]
        if first:
            key_acc[...] = jnp.zeros_like(key_acc)
            value_acc[...] = jnp.zeros_like(value_acc)
        else:
            key_acc[...] = carry_ref[:, :d]
            value_acc[...] = carry_ref[:, d:]

    def piece(at, column):
        ref, start = (kv_ref, at) if at < half else (kv_far_ref, at - half)
        return ref[start : start + chunk, column : column + d]

    pairs = scores_ref.shape[0]
    lanes = scores_ref.shape[2]
    heads = lanes // tokens
    chunks = range(0, seq, chunk)
    ahead = iota((tokens, lanes), 0) - (iota((tokens, lanes), 1) & (tokens - 1))
    limits = [(me - (me ^ offset)) * tokens for offset in offsets]

    def columns(pair, h):
        start = (pair * heads + h) * d
        return slice(start, start + d)

    def stacked(ref, pair):
        return jnp.concatenate([ref[:, columns(pair, h)] for h in range(heads)], axis=0)

    every = range(pairs)
    q = [stacked(q_ref, pair) for pair in every]
    g = [stacked(g_ref, pair) for pair in every]
    q_t = [jnp.transpose(value) for value in q]
    g_t = [jnp.transpose(value) for value in g]
    top, inverse, row_dot = {}, {}, {}

    def keep_rows(ref, pair, value):
        low = value.astype(BF16)
        for h in range(heads):
            ref[:, columns(pair, h)] = jnp.transpose(low[:, h * tokens : (h + 1) * tokens])

    def score_stage(pair):
        largest = jnp.full((1, lanes), -jnp.inf, F32)
        for at in chunks:
            scores = dot(piece(at, 0), q_t[pair])
            for part in range(0, chunk, tokens):
                allowed = ahead <= limits[(at + part) // tokens]
                some = jnp.where(allowed, scores[part : part + tokens], -jnp.inf)
                scores_ref[pair, at + part : at + part + tokens, :] = some
                largest = jnp.maximum(largest, jnp.max(some, axis=0, keepdims=True))
            yield
        top[pair] = largest * to_base2

    def raise_stage(pair):
        total = jnp.zeros((1, lanes), F32)
        for at in chunks:
            raised = jnp.exp2(scores_ref[pair, at : at + chunk, :] * to_base2 - top[pair])
            scores_ref[pair, at : at + chunk, :] = raised
            total = total + jnp.sum(raised, axis=0, keepdims=True)
            yield
        inverse[pair] = 1.0 / total

    def attend_stage(pair):
        attended = jnp.zeros((d, lanes), F32)
        for at in chunks:
            low = (scores_ref[pair, at : at + chunk, :] * inverse[pair]).astype(BF16)
            low_ref[pair, at : at + chunk, :] = low
            attended = attended + dot(value_t[:, at : at + chunk], low)
            value_acc[at : at + chunk, :] += dot(low, g[pair])
            yield
        keep_rows(out_ref, pair, attended)
        attended = attended.astype(BF16).astype(F32)
        row_dot[pair] = jnp.sum(g_t[pair].astype(F32) * attended, axis=0, keepdims=True)

    def back_stage(pair):
        query_back = jnp.zeros((d, lanes), F32)
        for at in chunks:
            low = low_ref[pair, at : at + chunk, :]
            prob_grad = dot(piece(at, d), g_t[pair])
            score_grad = (low.astype(F32) * (prob_grad - row_dot[pair])).astype(BF16)
            query_back = query_back + dot(key_t[:, at : at + chunk], score_grad)
            key_acc[at : at + chunk, :] += dot(score_grad, q[pair])
            yield
        keep_rows(qgrad_ref, pair, query_back * scale)

    stages = (score_stage, raise_stage, attend_stage, back_stage)
    for slot in range(pairs + len(stages) - 1):
        running = [stages[slot - pair](pair) for pair in every if 0 <= slot - pair < len(stages)]
        while running:
            running = [stage for stage in running if next(stage, True) is None]

    @pl.when(step == pl.num_programs(0) - 1)
    def _():
        if last:
            keep_ref[:, :d] = key_acc[:half, :] * scale
            keep_ref[:, d:] = value_acc[:half, :]
            send_ref[:, :d] = (key_acc[half:, :] * scale).astype(BF16)
            send_ref[:, d:] = value_acc[half:, :].astype(BF16)
        else:
            carried_ref[:, :d] = key_acc[...]
            carried_ref[:, d:] = value_acc[...]


def attention(me, offsets, queries, attn_grad, kv_near, kv_far, part, parts, carried=None):
    tokens, columns = queries.shape
    half, both = kv_near.shape
    seq = 2 * half
    heads = columns // HEAD_SIZE
    group = 4 if heads % (4 * parts) == 0 and seq <= 2048 else 2 if heads % (2 * parts) == 0 else 1
    pairs = PAIRS if heads % (group * PAIRS * parts) == 0 and seq <= 2048 else 1
    lanes = group * tokens
    chunk = min(CHUNK, half)
    steps = heads // (group * pairs * parts)
    first, last = part == 0, part == parts - 1
    tile = pl.BlockSpec((tokens, pairs * group * HEAD_SIZE), lambda i, m: (0, i + part * steps))
    whole = pl.BlockSpec((half, both), lambda i, m: (0, 0))
    sums = pl.BlockSpec((seq, both), lambda i, m: (0, 0))
    held = pl.BlockSpec(memory_space=pl.ANY)
    wide = jax.ShapeDtypeStruct(queries.shape, BF16)
    if last:
        final = [jax.ShapeDtypeStruct((half, both), F32), jax.ShapeDtypeStruct((half, both), BF16)]
    else:
        final = [jax.ShapeDtypeStruct((seq, both), F32)]
    return pl.pallas_call(
        functools.partial(attention_kernel, offsets, tokens, chunk, first, last),
        grid_spec=pltpu.PrefetchScalarGridSpec(
            num_scalar_prefetch=1,
            grid=(steps,),
            in_specs=[tile, tile, whole, whole] + ([] if first else [sums, held, held]),
            out_specs=[tile, tile] + ([whole, whole] if last else [sums]),
            scratch_shapes=[
                pltpu.VMEM((pairs, seq, lanes), F32),
                pltpu.VMEM((pairs, seq, lanes), BF16),
                pltpu.VMEM((HEAD_SIZE, seq), BF16),
                pltpu.VMEM((HEAD_SIZE, seq), BF16),
                pltpu.VMEM((seq, HEAD_SIZE), F32),
                pltpu.VMEM((seq, HEAD_SIZE), F32),
            ],
        ),
        out_shape=[wide, wide] + final,
        input_output_aliases={} if first else {6: 0, 7: 1},
        compiler_params=params(LARGE_VMEM),
        cost_estimate=cost(
            12 * tokens * columns * seq // parts,
            8 * tokens * columns // parts,
            tokens * heads * seq // parts,
        ),
        name="attention",
    )(me, in_hbm(queries), in_hbm(attn_grad), in_hbm(kv_near), kv_far, *(() if first else (carried[2], carried[0], carried[1])))


def swap(value, axis, bit):
    count = lax.axis_size(axis)
    return lax.ppermute(value, axis, [(i, i ^ bit) for i in range(count)])


def after(value, *earlier):
    return lax.optimization_barrier((value, *earlier))[0]


def far_bits(count):
    bits = []
    bit = count // 2
    while bit >= 1:
        bits.append(bit)
        bit //= 2
    return bits


def spread_sum(part, ctx_count, beside):
    result = None
    bit = 2
    while True:
        arrived = swap(part.astype(BF16), "ctx", bit)
        if result is None:
            result = beside(part)
            arrived = after(arrived, *result)
        bit *= 2
        if bit >= ctx_count:
            return (part, arrived), result
        part = part.astype(F32) + arrived.astype(F32)


def total_of(addends):
    return addends[0].astype(F32) + addends[1].astype(F32)


def activate(gate, up):
    return (jax.nn.silu(gate) * up).astype(BF16)


def gate_backward(hidden_grad, gate, up):
    s = jax.nn.sigmoid(gate)
    gate_back = (hidden_grad * up * s * (1.0 + gate * (1.0 - s))).astype(BF16)
    up_back = (hidden_grad * (gate * s)).astype(BF16)
    return jnp.stack([gate_back, up_back])


def body(
    queries, key_proj, value_matrix_rows, attn_grad, moe_input, moe_grad,
    expert_ids, route_weights, gate_proj, up_proj, down_proj,
):
    ctx_count = lax.axis_size("ctx")
    exp_count = lax.axis_size("exp")
    ctx_index = lax.axis_index("ctx")
    exp_index = lax.axis_index("exp")
    tokens = queries.shape[0]
    d = HEAD_SIZE
    kv_heads = key_proj.shape[1] // d
    sharers = ctx_count // kv_heads
    kv_head = ctx_index // sharers
    width = moe_input.shape[1]
    local = gate_proj.shape[0]
    expert_total = local * exp_count
    slot_count = 2 * ((tokens + expert_total - 2) // (expert_total - 1))
    slots = Slots(slot_count, width, exp_count, local)
    core = ctx_index % 2
    mine = core.astype(jnp.int32).reshape(1)
    other = 1 - mine
    order = jnp.concatenate([mine, other])
    shape = (exp_count, local, slots.rows, slots.columns)

    def exchange(rows):
        flat = rows.reshape(exp_count, local * slots.rows, slots.columns)
        return lax.all_to_all(flat, "exp", split_axis=0, concat_axis=0, tiled=True)

    me = exp_index.astype(jnp.int32).reshape(1)
    ids = expert_ids.T
    gains = route_weights.T

    kv = jnp.concatenate(
        [
            lax.dynamic_slice_in_dim(key_proj, kv_head * d, d, 1),
            lax.dynamic_slice_in_dim(value_matrix_rows, kv_head * d, d, 1),
        ],
        axis=1,
    )
    send_rows = dispatch(slots, False, ids, gains, moe_input)
    offsets = [0]
    kv_far = None
    for bit in far_bits(exp_count):
        if kv_far is not None:
            kv = jnp.concatenate([kv, after(kv_far, send_rows)], axis=0)
        if bit == 2:
            recv_rows = exchange(after(send_rows, kv)).reshape(shape)
        kv_far = swap(kv, "exp", bit)
        offsets = offsets + [o ^ bit for o in offsets]
    send_scaled = dispatch(slots, True, ids, gains, after(moe_grad, send_rows))
    held = hold(other, after(gate_proj, send_scaled), up_proj)

    def heads(part, carried, earlier):
        return attention(
            me, tuple(offsets), after(queries, earlier), attn_grad, kv, kv_far, part, 1, carried
        )

    recv_rows = after(recv_rows, kv)
    gu_send, held, rows = gate_up_send(slots, order[::-1], recv_rows, held, gate_proj, up_proj)
    gu_recv = swap(gu_send, "ctx", 1)
    gu_part = gate_up_keep(rows, held, gu_recv)
    recv_scaled = exchange(after(send_scaled, gu_part)).reshape(shape)
    gate_up_sum, (attn_out, query_grad, kv_keep, kv_send) = spread_sum(
        gu_part, ctx_count, lambda part: heads(0, None, part)
    )
    kv_recv = swap(kv_send, "exp", 1)
    hidden = activate(*total_of(gate_up_sum))
    hidden_other = swap(hidden, "ctx", 1)
    out_rows = route_out(slots, order, hidden, hidden_other, down_proj)
    back_out = exchange(out_rows).reshape(slots.total, slots.columns)

    hg_send, rows = hidden_grad_send(slots, order[::-1], after(recv_scaled, out_rows), down_proj)
    hg_recv = swap(hg_send, "ctx", 1)
    hg_part = hidden_grad_keep(mine, rows, down_proj, hg_recv)
    held = hold(mine, after(gate_proj, hg_part), up_proj)

    kv_sum = kv_keep + after(kv_recv, hg_part).astype(F32)
    kv_low = kv_sum.astype(BF16)
    blocks = exp_count // 2
    kv_parts = [
        swap(kv_low[i * tokens : (i + 1) * tokens], "exp", offsets[i]) for i in range(1, blocks)
    ]
    gate_up_sum = [after(value, hg_part) for value in gate_up_sum]
    gate_up_total = total_of(gate_up_sum)
    hg_sum, _ = spread_sum(hg_part, ctx_count, lambda part: (kv_low, gate_up_total, held))
    back = gate_backward(total_of(hg_sum), *gate_up_total)
    back_other = swap(back, "ctx", 1)
    in_rows = route_in(slots, order, back, back_other, held, gate_proj, up_proj)
    kv_total = kv_sum[:tokens]
    for part in kv_parts:
        kv_total = kv_total + after(part, in_rows).astype(F32)
    kv_total = kv_total.astype(BF16)
    back_in = exchange(after(in_rows, kv_total)).reshape(slots.total, slots.columns)

    moe_out = combine(slots, True, ids, gains, after(back_out, in_rows))
    input_grad = combine(slots, False, ids, gains, back_in)

    kv_every = lax.all_gather(after(kv_total, in_rows), "ctx", axis=0, tiled=False)
    if sharers > 1:
        kv_every = kv_every.astype(F32).reshape(kv_heads, sharers, tokens, 2 * d).sum(axis=1)
    kv_every = kv_every.astype(BF16)
    key_grad = jnp.concatenate([kv_every[h, :, :d] for h in range(kv_heads)], axis=1)
    value_grad = jnp.concatenate([kv_every[h, :, d:] for h in range(kv_heads)], axis=1)
    return (attn_out, query_grad, key_grad, value_grad, moe_out, input_grad)


def solution(mesh):
    placed = (
        P("exp", "ctx"),
        P("exp", None),
        P("exp", None),
        P("exp", "ctx"),
        P("exp", "ctx"),
        P("exp", "ctx"),
        P("exp", None),
        P("exp", None),
        P("exp", "ctx", None),
        P("exp", "ctx", None),
        P("exp", None, "ctx"),
    )
    return jax.shard_map(
        body,
        mesh=mesh,
        in_specs=placed,
        out_specs=(
            P("exp", "ctx"),
            P("exp", "ctx"),
            P("exp", None),
            P("exp", None),
            P("exp", "ctx"),
            P("exp", "ctx"),
        ),
        check_vma=False,
    )
```

```python
import functools
import math

import jax
import jax.numpy as jnp
from jax import lax
from jax.experimental import pallas as pl
from jax.experimental.pallas import tpu as pltpu
from jax.sharding import PartitionSpec as P

HEAD_SIZE = 128
LANES = 128
ROW_TILE = 16
PAIRS = 4
CHUNK = 512
OVERLAP_FLOPS = 2.25e9
SMALL_VMEM = 16 * 1024 * 1024
LARGE_VMEM = 20 * 1024 * 1024
EXPERT_VMEM = 16 * 1024 * 1024
BF16 = jnp.bfloat16
F32 = jnp.float32


def dot(a, b, a_dim=1, b_dim=0):
    return lax.dot_general(a, b, (((a_dim,), (b_dim,)), ((), ())), preferred_element_type=F32)


def iota(shape, dim):
    return lax.broadcasted_iota(jnp.int32, shape, dim)


def params(vmem_bytes):
    return pltpu.CompilerParams(vmem_limit_bytes=vmem_bytes, dimension_semantics=("arbitrary",))


def in_hbm(value):
    return pltpu.with_memory_space_constraint(value, pltpu.HBM)


def cost(flops, bytes_accessed, transcendentals=0):
    return pl.CostEstimate(
        flops=int(flops), bytes_accessed=int(bytes_accessed), transcendentals=int(transcendentals)
    )


def power_of_two(value):
    return value > 0 and value & (value - 1) == 0


class Slots:
    def __init__(self, slot_count, width, exp_count, local_experts):
        whole = slot_count // ROW_TILE * ROW_TILE
        rem = slot_count - whole
        blocks = width // LANES
        self.fold = (
            whole > 0
            and rem > 0
            and power_of_two(rem)
            and power_of_two(exp_count)
            and rem * blocks <= whole
            and (rem * exp_count) % ROW_TILE == 0
        )
        self.rows = whole if self.fold or rem == 0 else whole + ROW_TILE
        self.rem = rem if self.fold else 0
        self.blocks = blocks
        self.width = width
        self.columns = width + (LANES if self.fold else 0)
        self.exp_count = exp_count
        self.local = local_experts
        self.experts = exp_count * local_experts
        self.total = self.experts * self.rows
        self.per_expert = exp_count * (self.rows + self.rem)


def route_places(ids, slots):
    top, tokens = ids.shape
    expert = iota((-(-slots.experts // ROW_TILE) * ROW_TILE, tokens), 0)
    hits = [(ids[r : r + 1, :] == expert).astype(F32) for r in range(top)]
    earlier = (iota((tokens, tokens), 0) < iota((tokens, tokens), 1)).astype(BF16)
    before = dot(sum(hits).astype(BF16), earlier)
    found = []
    for r in range(top):
        rank = jnp.sum(hits[r] * before, axis=0, keepdims=True)
        base = ids[r : r + 1, :].astype(F32) * slots.rows
        inside = rank < slots.rows
        main = jnp.where(inside, base + rank, -1.0)
        folded = jnp.where(inside, -65536.0, base + rank - slots.rows)
        found.append((main, folded))
    return found


def as_column(row):
    tokens = row.shape[1]
    return jnp.transpose(jnp.broadcast_to(row, (LANES, tokens)))[:, 0:1]


def dispatch_kernel(slots, weighted, ids_ref, gain_ref, rows_ref, out_ref):
    top, tokens = ids_ref.shape
    places = route_places(ids_ref[...], slots)
    gains = [gain_ref[r : r + 1, :] for r in range(top)]
    slot = iota((slots.total, tokens), 0).astype(F32)
    rows = rows_ref[...]

    def picks(wanted):
        pick = jnp.zeros((slots.total, tokens), F32)
        gain = pick
        for r in range(top):
            here = slot == wanted[r]
            pick = jnp.where(here, 1.0, pick)
            gain = jnp.where(here, gains[r], gain)
        return pick.astype(BF16), gain

    pick, gain = picks([main for main, _ in places])
    taken = dot(pick, rows)
    if weighted:
        taken = taken * jnp.sum(gain, axis=1, keepdims=True)
    out_ref[:, : slots.width] = taken.astype(BF16)
    if slots.fold:
        taken = jnp.zeros((slots.total, LANES), F32)
        total_gain = jnp.zeros((slots.total, tokens), F32)
        for f in range(slots.blocks):
            pick, gain = picks([start + float(f * slots.rem) for _, start in places])
            taken = taken + dot(pick, rows[:, f * LANES : (f + 1) * LANES])
            total_gain = total_gain + gain
        if weighted:
            taken = taken * jnp.sum(total_gain, axis=1, keepdims=True)
        out_ref[:, slots.width :] = taken.astype(BF16)


def dispatch(slots, weighted, ids, gains, rows):
    return pl.pallas_call(
        functools.partial(dispatch_kernel, slots, weighted),
        out_shape=jax.ShapeDtypeStruct((slots.total, slots.columns), BF16),
        compiler_params=pltpu.CompilerParams(vmem_limit_bytes=LARGE_VMEM),
        cost_estimate=cost(4 * slots.total * LANES * slots.width, 4 * slots.total * slots.columns),
        name="dispatch_scaled" if weighted else "dispatch_rows",
    )(in_hbm(ids), in_hbm(gains), in_hbm(rows))


def combine_kernel(slots, weighted, ids_ref, gain_ref, back_ref, out_ref):
    top, tokens = ids_ref.shape
    places = [
        (as_column(main), as_column(start))
        for main, start in route_places(ids_ref[...], slots)
    ]
    gains = [as_column(gain_ref[r : r + 1, :]) if weighted else 1.0 for r in range(top)]
    slot = iota((tokens, slots.total), 1).astype(F32)

    def table(wanted):
        found = jnp.zeros((tokens, slots.total), F32)
        for r in range(top):
            found = jnp.where(slot == wanted[r], gains[r], found)
        return found

    def apply(found, rows):
        high = found.astype(BF16)
        result = dot(high, rows)
        if weighted:
            result = result + dot((found - high.astype(F32)).astype(BF16), rows)
        return result

    result = apply(table([main for main, _ in places]), back_ref[:, : slots.width])
    if slots.fold:
        folded = back_ref[:, slots.width :]
        extra = [
            apply(table([start + float(f * slots.rem) for _, start in places]), folded)
            for f in range(slots.blocks)
        ]
        result = result + jnp.concatenate(extra, axis=1)
    out_ref[...] = result.astype(BF16)


def combine(slots, weighted, ids, gains, back):
    tokens = ids.shape[1]
    return pl.pallas_call(
        functools.partial(combine_kernel, slots, weighted),
        out_shape=jax.ShapeDtypeStruct((tokens, slots.width), BF16),
        compiler_params=pltpu.CompilerParams(vmem_limit_bytes=SMALL_VMEM),
        cost_estimate=cost(OVERLAP_FLOPS if weighted else 1e7, 4 * slots.total * slots.columns),
        name="combine_out" if weighted else "combine_in",
    )(ids, gains, back)


def fold_table(slots, shape, folded_dim):
    folded = iota(shape, folded_dim)
    plain = iota(shape, 1 - folded_dim)
    rem_bits = int(math.log2(slots.rem))
    exp_bits = int(math.log2(slots.exp_count))
    j = plain & (slots.rem - 1)
    source = (plain >> rem_bits) & (slots.exp_count - 1)
    f = plain >> (rem_bits + exp_bits)
    return (folded == source * slots.rows + f * slots.rem + j).astype(F32).astype(BF16)


def unpack_rows(slots, block):
    flat = block.reshape(slots.exp_count * slots.rows, slots.columns)
    if not slots.fold:
        return flat
    each = slots.exp_count * slots.rem
    plain = dot(
        fold_table(slots, (slots.blocks * each, slots.exp_count * slots.rows), 1),
        flat[:, slots.width :],
    ).astype(BF16)
    extra = jnp.concatenate(
        [plain[f * each : (f + 1) * each] for f in range(slots.blocks)], axis=1
    )
    return jnp.concatenate([flat[:, : slots.width], extra], axis=0)


def pack_rows(slots, rows, out_ref):
    count = slots.exp_count * slots.rows
    main = rows[:count].reshape(slots.exp_count, slots.rows, slots.width)
    out_ref[:, :, : slots.width] = main
    if slots.fold:
        each = slots.exp_count * slots.rem
        stacked = jnp.concatenate(
            [rows[count:, f * LANES : (f + 1) * LANES] for f in range(slots.blocks)], axis=0
        )
        folded = dot(fold_table(slots, (count, slots.blocks * each), 0), stacked).astype(BF16)
        out_ref[:, :, slots.width :] = folded.reshape(slots.exp_count, slots.rows, LANES)


def fetch(sources, targets, sems):
    copies = [
        pltpu.make_async_copy(source, target, sems.at[i])
        for i, (source, target) in enumerate(zip(sources, targets))
    ]
    for copy in copies:
        copy.start()
    return copies


def hold_kernel(expert_ref, gate_ref, up_ref, out_ref, sems):
    e = expert_ref[0]
    for copy in fetch([gate_ref.at[e], up_ref.at[e]], [out_ref.at[0], out_ref.at[1]], sems):
        copy.wait()


def hold(expert, gate_proj, up_proj):
    return expert_call(
        hold_kernel, "hold_weights", pltpu.VMEM((2, *gate_proj.shape[1:]), BF16), expert,
        in_hbm(gate_proj), in_hbm(up_proj), anywhere=(0, 1), copies=2,
    )


def expert_call(kernel, name, out_shape, scalars, *operands, anywhere=(), copies=0, held=None):
    in_vmem = pl.BlockSpec(memory_space=pltpu.VMEM)
    specs = [
        pl.BlockSpec(memory_space=pl.ANY) if i in anywhere else in_vmem
        for i in range(len(operands))
    ]
    if scalars is not None:
        specs = [pl.BlockSpec(memory_space=pltpu.SMEM)] + specs
        operands = (scalars, *operands)
    scratch = [] if held is None else [pltpu.VMEM(held, BF16)]
    if copies:
        scratch.append(pltpu.SemaphoreType.DMA((copies,)))
    return pl.pallas_call(
        kernel,
        in_specs=specs,
        out_specs=[in_vmem] * len(out_shape) if isinstance(out_shape, list) else in_vmem,
        out_shape=out_shape,
        scratch_shapes=scratch,
        compiler_params=pltpu.CompilerParams(vmem_limit_bytes=EXPERT_VMEM),
        name=name,
    )(*operands)


def gate_up_send_kernel(
    slots, order_ref, recv_ref, held_ref, gate_ref, up_ref, out_ref, next_ref, rows_ref, all_ref, sems
):
    e, following = order_ref[0], order_ref[1]
    copies = fetch(
        [recv_ref, gate_ref.at[following], up_ref.at[following]],
        [all_ref, next_ref.at[0], next_ref.at[1]],
        sems,
    )
    copies[0].wait()
    rows = unpack_rows(slots, all_ref[:, e])
    out_ref[0] = dot(rows, held_ref[0]).astype(BF16)
    out_ref[1] = dot(rows, held_ref[1]).astype(BF16)
    rows_ref[...] = unpack_rows(slots, all_ref[:, following])
    for copy in copies[1:]:
        copy.wait()


def gate_up_send(slots, order, recv, held, gate_proj, up_proj):
    out = [
        jax.ShapeDtypeStruct((2, slots.per_expert, gate_proj.shape[2]), BF16),
        pltpu.VMEM(held.shape, BF16),
        jax.ShapeDtypeStruct((slots.per_expert, slots.width), BF16),
    ]
    return expert_call(
        functools.partial(gate_up_send_kernel, slots), "gate_up_send", out, order,
        in_hbm(recv), held, in_hbm(gate_proj), in_hbm(up_proj),
        anywhere=(0, 2, 3), copies=3, held=recv.shape,
    )


def gate_up_keep_kernel(rows_ref, held_ref, arrived_ref, out_ref):
    for i in range(2):
        part = dot(rows_ref[...], held_ref[i]) + arrived_ref[i].astype(F32)
        out_ref[i] = part.astype(BF16)


def gate_up_keep(rows, held, arrived):
    out = jax.ShapeDtypeStruct(arrived.shape, BF16)
    return expert_call(gate_up_keep_kernel, "gate_up_keep", out, None, rows, held, arrived)


def hidden_grad_send_kernel(slots, order_ref, recv_ref, down_ref, out_ref, rows_ref):
    rows = unpack_rows(slots, recv_ref[:, order_ref[0]])
    out_ref[...] = dot(rows, down_ref[order_ref[0]], 1, 1).astype(BF16)
    rows_ref[...] = unpack_rows(slots, recv_ref[:, order_ref[1]])


def hidden_grad_send(slots, order, recv, down_proj):
    out = [
        jax.ShapeDtypeStruct((slots.per_expert, down_proj.shape[1]), BF16),
        jax.ShapeDtypeStruct((slots.per_expert, slots.width), BF16),
    ]
    kernel = functools.partial(hidden_grad_send_kernel, slots)
    return expert_call(kernel, "hidden_grad_send", out, order, recv, down_proj)


def hidden_grad_keep_kernel(expert_ref, rows_ref, down_ref, arrived_ref, out_ref):
    part = dot(rows_ref[...], down_ref[expert_ref[0]], 1, 1) + arrived_ref[...].astype(F32)
    out_ref[...] = part.astype(BF16)


def hidden_grad_keep(expert, rows, down_proj, arrived):
    out = jax.ShapeDtypeStruct(arrived.shape, BF16)
    return expert_call(
        hidden_grad_keep_kernel, "hidden_grad_keep", out, expert, rows, down_proj, arrived
    )


def store_rows(slots, rows, expert, packed_ref, out_ref, sem):
    pack_rows(slots, rows, packed_ref)
    copy = pltpu.make_async_copy(packed_ref, out_ref.at[:, expert], sem)
    copy.start()
    return copy


def packed_shape(slots):
    return (slots.exp_count, slots.local, slots.rows, slots.columns)


def packed_scratch(slots):
    return pltpu.VMEM((slots.local, slots.exp_count, slots.rows, slots.columns), BF16)


def route_out_kernel(slots, order_ref, mine_ref, other_ref, down_ref, out_ref, packed_ref, sems):
    stores = []
    for at, hidden_ref in enumerate((mine_ref, other_ref)):
        e = order_ref[at]
        rows = dot(hidden_ref[...], down_ref[e]).astype(BF16)
        stores.append(store_rows(slots, rows, e, packed_ref.at[at], out_ref, sems.at[at]))
    for store in stores:
        store.wait()


def route_out(slots, order, mine, other, down_proj):
    in_vmem = pl.BlockSpec(memory_space=pltpu.VMEM)
    return pl.pallas_call(
        functools.partial(route_out_kernel, slots),
        in_specs=[pl.BlockSpec(memory_space=pltpu.SMEM), in_vmem, in_vmem, in_vmem],
        out_specs=pl.BlockSpec(memory_space=pltpu.HBM),
        out_shape=pltpu.HBM(packed_shape(slots), BF16),
        scratch_shapes=[packed_scratch(slots), pltpu.SemaphoreType.DMA((slots.local,))],
        compiler_params=pltpu.CompilerParams(vmem_limit_bytes=EXPERT_VMEM),
        name="route_out",
    )(order, mine, other, down_proj)


def route_in_kernel(
    slots, order_ref, mine_ref, other_ref, held_ref, gate_ref, up_ref, out_ref,
    mine_held, other_held, next_ref, packed_ref, sems, out_sems,
):
    first, second = order_ref[0], order_ref[1]
    copies = fetch(
        [mine_ref, gate_ref.at[second], up_ref.at[second], other_ref],
        [mine_held, next_ref.at[0], next_ref.at[1], other_held],
        sems,
    )
    copies[0].wait()
    total = dot(mine_held[0], held_ref[0], 1, 1) + dot(mine_held[1], held_ref[1], 1, 1)
    rows = total.astype(BF16)
    stores = [store_rows(slots, rows, first, packed_ref.at[0], out_ref, out_sems.at[0])]
    for copy in copies[1:]:
        copy.wait()
    total = dot(other_held[0], next_ref[0], 1, 1) + dot(other_held[1], next_ref[1], 1, 1)
    rows = total.astype(BF16)
    stores.append(store_rows(slots, rows, second, packed_ref.at[1], out_ref, out_sems.at[1]))
    for store in stores:
        store.wait()


def route_in(slots, order, mine, other, held, gate_proj, up_proj):
    anywhere = pl.BlockSpec(memory_space=pl.ANY)
    return pl.pallas_call(
        functools.partial(route_in_kernel, slots),
        in_specs=[
            pl.BlockSpec(memory_space=pltpu.SMEM), anywhere, anywhere,
            pl.BlockSpec(memory_space=pltpu.VMEM), anywhere, anywhere,
        ],
        out_specs=pl.BlockSpec(memory_space=pltpu.HBM),
        out_shape=pltpu.HBM(packed_shape(slots), BF16),
        scratch_shapes=[
            pltpu.VMEM(mine.shape, BF16),
            pltpu.VMEM(other.shape, BF16),
            pltpu.VMEM(held.shape, BF16),
            packed_scratch(slots),
            pltpu.SemaphoreType.DMA((4,)),
            pltpu.SemaphoreType.DMA((slots.local,)),
        ],
        compiler_params=pltpu.CompilerParams(vmem_limit_bytes=EXPERT_VMEM),
        name="route_in",
    )(order, mine, other, held, in_hbm(gate_proj), in_hbm(up_proj))


def attention_kernel(offsets, tokens, chunk, first, last, me_ref, q_ref, g_ref, kv_ref, kv_far_ref, *refs):
    if not first:
        carry_ref, refs = refs[0], refs[3:]
    out_ref, qgrad_ref = refs[:2]
    if last:
        keep_ref, send_ref = refs[2:4]
    else:
        carried_ref = refs[2]
    scores_ref, low_ref, key_t, value_t, key_acc, value_acc = refs[-6:]
    d = HEAD_SIZE
    step = pl.program_id(0)
    me = me_ref[0]
    half = kv_ref.shape[0]
    seq = 2 * half
    scale = d ** (-0.5)
    to_base2 = scale * math.log2(math.e)

    @pl.when(step == 0)
    def _():
        for start, ref in ((0, kv_ref), (half, kv_far_ref)):
            for at in range(0, half, tokens):
                both = jnp.transpose(ref[at : at + tokens, :])
                key_t[:, start + at : start + at + tokens] = both[:d]
                value_t[:, start + at : start + at + tokens] = both[d:]
        if first:
            key_acc[...] = jnp.zeros_like(key_acc)
            value_acc[...] = jnp.zeros_like(value_acc)
        else:
            key_acc[...] = carry_ref[:, :d]
            value_acc[...] = carry_ref[:, d:]

    def piece(at, column):
        ref, start = (kv_ref, at) if at < half else (kv_far_ref, at - half)
        return ref[start : start + chunk, column : column + d]

    pairs = scores_ref.shape[0]
    lanes = scores_ref.shape[2]
    heads = lanes // tokens
    chunks = range(0, seq, chunk)
    ahead = iota((tokens, lanes), 0) - (iota((tokens, lanes), 1) & (tokens - 1))
    limits = [(me - (me ^ offset)) * tokens for offset in offsets]

    def columns(pair, h):
        start = (pair * heads + h) * d
        return slice(start, start + d)

    def stacked(ref, pair):
        return jnp.concatenate([ref[:, columns(pair, h)] for h in range(heads)], axis=0)

    every = range(pairs)
    q = [stacked(q_ref, pair) for pair in every]
    g = [stacked(g_ref, pair) for pair in every]
    q_t = [jnp.transpose(value) for value in q]
    g_t = [jnp.transpose(value) for value in g]
    top, inverse, row_dot = {}, {}, {}

    def keep_rows(ref, pair, value):
        low = value.astype(BF16)
        for h in range(heads):
            ref[:, columns(pair, h)] = jnp.transpose(low[:, h * tokens : (h + 1) * tokens])

    def score_stage(pair):
        largest = jnp.full((1, lanes), -jnp.inf, F32)
        for at in chunks:
            scores = dot(piece(at, 0), q_t[pair])
            for part in range(0, chunk, tokens):
                allowed = ahead <= limits[(at + part) // tokens]
                some = jnp.where(allowed, scores[part : part + tokens], -jnp.inf)
                scores_ref[pair, at + part : at + part + tokens, :] = some
                largest = jnp.maximum(largest, jnp.max(some, axis=0, keepdims=True))
            yield
        top[pair] = largest * to_base2

    def raise_stage(pair):
        total = jnp.zeros((1, lanes), F32)
        for at in chunks:
            raised = jnp.exp2(scores_ref[pair, at : at + chunk, :] * to_base2 - top[pair])
            scores_ref[pair, at : at + chunk, :] = raised
            total = total + jnp.sum(raised, axis=0, keepdims=True)
            yield
        inverse[pair] = 1.0 / total

    def attend_stage(pair):
        attended = jnp.zeros((d, lanes), F32)
        for at in chunks:
            low = (scores_ref[pair, at : at + chunk, :] * inverse[pair]).astype(BF16)
            low_ref[pair, at : at + chunk, :] = low
            attended = attended + dot(value_t[:, at : at + chunk], low)
            value_acc[at : at + chunk, :] += dot(low, g[pair])
            yield
        keep_rows(out_ref, pair, attended)
        attended = attended.astype(BF16).astype(F32)
        row_dot[pair] = jnp.sum(g_t[pair].astype(F32) * attended, axis=0, keepdims=True)

    def back_stage(pair):
        query_back = jnp.zeros((d, lanes), F32)
        for at in chunks:
            low = low_ref[pair, at : at + chunk, :]
            prob_grad = dot(piece(at, d), g_t[pair])
            score_grad = (low.astype(F32) * (prob_grad - row_dot[pair])).astype(BF16)
            query_back = query_back + dot(key_t[:, at : at + chunk], score_grad)
            key_acc[at : at + chunk, :] += dot(score_grad, q[pair])
            yield
        keep_rows(qgrad_ref, pair, query_back * scale)

    stages = (score_stage, raise_stage, attend_stage, back_stage)
    for slot in range(pairs + len(stages) - 1):
        running = [stages[slot - pair](pair) for pair in every if 0 <= slot - pair < len(stages)]
        while running:
            running = [stage for stage in running if next(stage, True) is None]

    @pl.when(step == pl.num_programs(0) - 1)
    def _():
        if last:
            keep_ref[:, :d] = key_acc[:half, :] * scale
            keep_ref[:, d:] = value_acc[:half, :]
            send_ref[:, :d] = (key_acc[half:, :] * scale).astype(BF16)
            send_ref[:, d:] = value_acc[half:, :].astype(BF16)
        else:
            carried_ref[:, :d] = key_acc[...]
            carried_ref[:, d:] = value_acc[...]


def attention(me, offsets, queries, attn_grad, kv_near, kv_far, part, parts, carried=None):
    tokens, columns = queries.shape
    half, both = kv_near.shape
    seq = 2 * half
    heads = columns // HEAD_SIZE
    group = 4 if heads % (4 * parts) == 0 and seq <= 2048 else 2 if heads % (2 * parts) == 0 else 1
    pairs = PAIRS if heads % (group * PAIRS * parts) == 0 and seq <= 2048 else 1
    lanes = group * tokens
    chunk = min(CHUNK, half)
    steps = heads // (group * pairs * parts)
    first, last = part == 0, part == parts - 1
    tile = pl.BlockSpec((tokens, pairs * group * HEAD_SIZE), lambda i, m: (0, i + part * steps))
    whole = pl.BlockSpec((half, both), lambda i, m: (0, 0))
    sums = pl.BlockSpec((seq, both), lambda i, m: (0, 0))
    held = pl.BlockSpec(memory_space=pl.ANY)
    wide = jax.ShapeDtypeStruct(queries.shape, BF16)
    if last:
        final = [jax.ShapeDtypeStruct((half, both), F32), jax.ShapeDtypeStruct((half, both), BF16)]
    else:
        final = [jax.ShapeDtypeStruct((seq, both), F32)]
    return pl.pallas_call(
        functools.partial(attention_kernel, offsets, tokens, chunk, first, last),
        grid_spec=pltpu.PrefetchScalarGridSpec(
            num_scalar_prefetch=1,
            grid=(steps,),
            in_specs=[tile, tile, whole, whole] + ([] if first else [sums, held, held]),
            out_specs=[tile, tile] + ([whole, whole] if last else [sums]),
            scratch_shapes=[
                pltpu.VMEM((pairs, seq, lanes), F32),
                pltpu.VMEM((pairs, seq, lanes), BF16),
                pltpu.VMEM((HEAD_SIZE, seq), BF16),
                pltpu.VMEM((HEAD_SIZE, seq), BF16),
                pltpu.VMEM((seq, HEAD_SIZE), F32),
                pltpu.VMEM((seq, HEAD_SIZE), F32),
            ],
        ),
        out_shape=[wide, wide] + final,
        input_output_aliases={} if first else {6: 0, 7: 1},
        compiler_params=params(LARGE_VMEM),
        cost_estimate=cost(
            12 * tokens * columns * seq // parts,
            8 * tokens * columns // parts,
            tokens * heads * seq // parts,
        ),
        name="attention",
    )(me, in_hbm(queries), in_hbm(attn_grad), in_hbm(kv_near), kv_far, *(() if first else (carried[2], carried[0], carried[1])))


def swap(value, axis, bit):
    count = lax.axis_size(axis)
    return lax.ppermute(value, axis, [(i, i ^ bit) for i in range(count)])


def after(value, *earlier):
    return lax.optimization_barrier((value, *earlier))[0]


def far_bits(count):
    bits = []
    bit = count // 2
    while bit >= 1:
        bits.append(bit)
        bit //= 2
    return bits


def spread_sum(part, ctx_count, beside):
    result = None
    bit = 2
    while True:
        arrived = swap(part.astype(BF16), "ctx", bit)
        if result is None:
            result = beside(part)
            arrived = after(arrived, *result)
        bit *= 2
        if bit >= ctx_count:
            return (part, arrived), result
        part = part.astype(F32) + arrived.astype(F32)


def total_of(addends):
    return addends[0].astype(F32) + addends[1].astype(F32)


def activate(gate, up):
    return (jax.nn.silu(gate) * up).astype(BF16)


def gate_backward(hidden_grad, gate, up):
    s = jax.nn.sigmoid(gate)
    gate_back = (hidden_grad * up * s * (1.0 + gate * (1.0 - s))).astype(BF16)
    up_back = (hidden_grad * (gate * s)).astype(BF16)
    return jnp.stack([gate_back, up_back])


def body(
    queries, key_proj, value_matrix_rows, attn_grad, moe_input, moe_grad,
    expert_ids, route_weights, gate_proj, up_proj, down_proj,
):
    ctx_count = lax.axis_size("ctx")
    exp_count = lax.axis_size("exp")
    ctx_index = lax.axis_index("ctx")
    exp_index = lax.axis_index("exp")
    tokens = queries.shape[0]
    d = HEAD_SIZE
    kv_heads = key_proj.shape[1] // d
    sharers = ctx_count // kv_heads
    kv_head = ctx_index // sharers
    width = moe_input.shape[1]
    local = gate_proj.shape[0]
    expert_total = local * exp_count
    slot_count = 2 * ((tokens + expert_total - 2) // (expert_total - 1))
    slots = Slots(slot_count, width, exp_count, local)
    core = ctx_index % 2
    mine = core.astype(jnp.int32).reshape(1)
    other = 1 - mine
    order = jnp.concatenate([mine, other])
    shape = (exp_count, local, slots.rows, slots.columns)

    def exchange(rows):
        flat = rows.reshape(exp_count, local * slots.rows, slots.columns)
        return lax.all_to_all(flat, "exp", split_axis=0, concat_axis=0, tiled=True)

    me = exp_index.astype(jnp.int32).reshape(1)
    ids = expert_ids.T
    gains = route_weights.T

    kv = jnp.concatenate(
        [
            lax.dynamic_slice_in_dim(key_proj, kv_head * d, d, 1),
            lax.dynamic_slice_in_dim(value_matrix_rows, kv_head * d, d, 1),
        ],
        axis=1,
    )
    send_rows = dispatch(slots, False, ids, gains, moe_input)
    offsets = [0]
    kv_far = None
    for bit in far_bits(exp_count):
        if kv_far is not None:
            kv = jnp.concatenate([kv, after(kv_far, send_rows)], axis=0)
        if bit == 2:
            recv_rows = exchange(after(send_rows, kv)).reshape(shape)
        kv_far = swap(kv, "exp", bit)
        offsets = offsets + [o ^ bit for o in offsets]
    send_scaled = dispatch(slots, True, ids, gains, after(moe_grad, send_rows))
    held = hold(other, after(gate_proj, send_scaled), up_proj)

    def heads(part, carried, earlier):
        return attention(
            me, tuple(offsets), after(queries, earlier), attn_grad, kv, kv_far, part, 1, carried
        )

    recv_rows = after(recv_rows, kv)
    gu_send, held, rows = gate_up_send(slots, order[::-1], recv_rows, held, gate_proj, up_proj)
    gu_recv = swap(gu_send, "ctx", 1)
    gu_part = gate_up_keep(rows, held, gu_recv)
    recv_scaled = exchange(after(send_scaled, gu_part)).reshape(shape)
    gate_up_sum, (attn_out, query_grad, kv_keep, kv_send) = spread_sum(
        gu_part, ctx_count, lambda part: heads(0, None, part)
    )
    kv_recv = swap(kv_send, "exp", 1)
    hidden = activate(*total_of(gate_up_sum))
    hidden_other = swap(hidden, "ctx", 1)
    out_rows = route_out(slots, order, hidden, hidden_other, down_proj)
    back_out = exchange(out_rows).reshape(slots.total, slots.columns)

    hg_send, rows = hidden_grad_send(slots, order[::-1], after(recv_scaled, out_rows), down_proj)
    hg_recv = swap(hg_send, "ctx", 1)
    hg_part = hidden_grad_keep(mine, rows, down_proj, hg_recv)
    held = hold(mine, after(gate_proj, hg_part), up_proj)

    kv_sum = kv_keep + after(kv_recv, hg_part).astype(F32)
    kv_low = kv_sum.astype(BF16)
    blocks = exp_count // 2
    kv_parts = [
        swap(kv_low[i * tokens : (i + 1) * tokens], "exp", offsets[i]) for i in range(1, blocks)
    ]
    gate_up_sum = [after(value, hg_part) for value in gate_up_sum]
    gate_up_total = total_of(gate_up_sum)
    hg_sum, _ = spread_sum(hg_part, ctx_count, lambda part: (kv_low, gate_up_total, held))
    back = gate_backward(total_of(hg_sum), *gate_up_total)
    back_other = swap(back, "ctx", 1)
    in_rows = route_in(slots, order, back, back_other, held, gate_proj, up_proj)
    kv_total = kv_sum[:tokens]
    for part in kv_parts:
        kv_total = kv_total + after(part, in_rows).astype(F32)
    kv_total = kv_total.astype(BF16)
    back_in = exchange(in_rows).reshape(slots.total, slots.columns)

    moe_out = combine(slots, True, ids, gains, after(back_out, kv_total))
    input_grad = combine(slots, False, ids, gains, back_in)

    kv_every = lax.all_gather(after(kv_total, in_rows), "ctx", axis=0, tiled=False)
    if sharers > 1:
        kv_every = kv_every.astype(F32).reshape(kv_heads, sharers, tokens, 2 * d).sum(axis=1)
    kv_every = kv_every.astype(BF16)
    key_grad = jnp.concatenate([kv_every[h, :, :d] for h in range(kv_heads)], axis=1)
    value_grad = jnp.concatenate([kv_every[h, :, d:] for h in range(kv_heads)], axis=1)
    return (attn_out, query_grad, key_grad, value_grad, moe_out, input_grad)


def solution(mesh):
    placed = (
        P("exp", "ctx"),
        P("exp", None),
        P("exp", None),
        P("exp", "ctx"),
        P("exp", "ctx"),
        P("exp", "ctx"),
        P("exp", None),
        P("exp", None),
        P("exp", "ctx", None),
        P("exp", "ctx", None),
        P("exp", None, "ctx"),
    )
    return jax.shard_map(
        body,
        mesh=mesh,
        in_specs=placed,
        out_specs=(
            P("exp", "ctx"),
            P("exp", "ctx"),
            P("exp", None),
            P("exp", None),
            P("exp", "ctx"),
            P("exp", "ctx"),
        ),
        check_vma=False,
    )
```

```python
import functools
import math

import jax
import jax.numpy as jnp
from jax import lax
from jax.experimental import pallas as pl
from jax.experimental.pallas import tpu as pltpu
from jax.sharding import PartitionSpec as P

HEAD_SIZE = 128
LANES = 128
ROW_TILE = 16
PAIRS = 4
CHUNK = 512
OVERLAP_FLOPS = 2.25e9
SMALL_VMEM = 16 * 1024 * 1024
LARGE_VMEM = 20 * 1024 * 1024
EXPERT_VMEM = 16 * 1024 * 1024
BF16 = jnp.bfloat16
F32 = jnp.float32


def dot(a, b, a_dim=1, b_dim=0):
    return lax.dot_general(a, b, (((a_dim,), (b_dim,)), ((), ())), preferred_element_type=F32)


def iota(shape, dim):
    return lax.broadcasted_iota(jnp.int32, shape, dim)


def params(vmem_bytes):
    return pltpu.CompilerParams(vmem_limit_bytes=vmem_bytes, dimension_semantics=("arbitrary",))


def in_hbm(value):
    return pltpu.with_memory_space_constraint(value, pltpu.HBM)


def cost(flops, bytes_accessed, transcendentals=0):
    return pl.CostEstimate(
        flops=int(flops), bytes_accessed=int(bytes_accessed), transcendentals=int(transcendentals)
    )


def power_of_two(value):
    return value > 0 and value & (value - 1) == 0


class Slots:
    def __init__(self, slot_count, width, exp_count, local_experts):
        whole = slot_count // ROW_TILE * ROW_TILE
        rem = slot_count - whole
        blocks = width // LANES
        self.fold = (
            whole > 0
            and rem > 0
            and power_of_two(rem)
            and power_of_two(exp_count)
            and rem * blocks <= whole
            and (rem * exp_count) % ROW_TILE == 0
        )
        self.rows = whole if self.fold or rem == 0 else whole + ROW_TILE
        self.rem = rem if self.fold else 0
        self.blocks = blocks
        self.width = width
        self.columns = width + (LANES if self.fold else 0)
        self.exp_count = exp_count
        self.local = local_experts
        self.experts = exp_count * local_experts
        self.total = self.experts * self.rows
        self.per_expert = exp_count * (self.rows + self.rem)


def route_places(ids, slots):
    top, tokens = ids.shape
    expert = iota((-(-slots.experts // ROW_TILE) * ROW_TILE, tokens), 0)
    hits = [(ids[r : r + 1, :] == expert).astype(F32) for r in range(top)]
    earlier = (iota((tokens, tokens), 0) < iota((tokens, tokens), 1)).astype(BF16)
    before = dot(sum(hits).astype(BF16), earlier)
    found = []
    for r in range(top):
        rank = jnp.sum(hits[r] * before, axis=0, keepdims=True)
        base = ids[r : r + 1, :].astype(F32) * slots.rows
        inside = rank < slots.rows
        main = jnp.where(inside, base + rank, -1.0)
        folded = jnp.where(inside, -65536.0, base + rank - slots.rows)
        found.append((main, folded))
    return found


def as_column(row):
    tokens = row.shape[1]
    return jnp.transpose(jnp.broadcast_to(row, (LANES, tokens)))[:, 0:1]


def dispatch_kernel(slots, weighted, ids_ref, gain_ref, rows_ref, out_ref):
    top, tokens = ids_ref.shape
    places = route_places(ids_ref[...], slots)
    gains = [gain_ref[r : r + 1, :] for r in range(top)]
    slot = iota((slots.total, tokens), 0).astype(F32)
    rows = rows_ref[...]

    def picks(wanted):
        pick = jnp.zeros((slots.total, tokens), F32)
        gain = pick
        for r in range(top):
            here = slot == wanted[r]
            pick = jnp.where(here, 1.0, pick)
            gain = jnp.where(here, gains[r], gain)
        return pick.astype(BF16), gain

    pick, gain = picks([main for main, _ in places])
    taken = dot(pick, rows)
    if weighted:
        taken = taken * jnp.sum(gain, axis=1, keepdims=True)
    out_ref[:, : slots.width] = taken.astype(BF16)
    if slots.fold:
        taken = jnp.zeros((slots.total, LANES), F32)
        total_gain = jnp.zeros((slots.total, tokens), F32)
        for f in range(slots.blocks):
            pick, gain = picks([start + float(f * slots.rem) for _, start in places])
            taken = taken + dot(pick, rows[:, f * LANES : (f + 1) * LANES])
            total_gain = total_gain + gain
        if weighted:
            taken = taken * jnp.sum(total_gain, axis=1, keepdims=True)
        out_ref[:, slots.width :] = taken.astype(BF16)


def dispatch(slots, weighted, ids, gains, rows):
    return pl.pallas_call(
        functools.partial(dispatch_kernel, slots, weighted),
        out_shape=jax.ShapeDtypeStruct((slots.total, slots.columns), BF16),
        compiler_params=pltpu.CompilerParams(vmem_limit_bytes=LARGE_VMEM),
        cost_estimate=cost(4 * slots.total * LANES * slots.width, 4 * slots.total * slots.columns),
        name="dispatch_scaled" if weighted else "dispatch_rows",
    )(in_hbm(ids), in_hbm(gains), in_hbm(rows))


def combine_kernel(slots, weighted, ids_ref, gain_ref, back_ref, out_ref):
    top, tokens = ids_ref.shape
    places = [
        (as_column(main), as_column(start))
        for main, start in route_places(ids_ref[...], slots)
    ]
    gains = [as_column(gain_ref[r : r + 1, :]) if weighted else 1.0 for r in range(top)]
    slot = iota((tokens, slots.total), 1).astype(F32)

    def table(wanted):
        found = jnp.zeros((tokens, slots.total), F32)
        for r in range(top):
            found = jnp.where(slot == wanted[r], gains[r], found)
        return found

    def apply(found, rows):
        high = found.astype(BF16)
        result = dot(high, rows)
        if weighted:
            result = result + dot((found - high.astype(F32)).astype(BF16), rows)
        return result

    result = apply(table([main for main, _ in places]), back_ref[:, : slots.width])
    if slots.fold:
        folded = back_ref[:, slots.width :]
        extra = [
            apply(table([start + float(f * slots.rem) for _, start in places]), folded)
            for f in range(slots.blocks)
        ]
        result = result + jnp.concatenate(extra, axis=1)
    out_ref[...] = result.astype(BF16)


def combine(slots, weighted, ids, gains, back):
    tokens = ids.shape[1]
    return pl.pallas_call(
        functools.partial(combine_kernel, slots, weighted),
        out_shape=jax.ShapeDtypeStruct((tokens, slots.width), BF16),
        compiler_params=pltpu.CompilerParams(vmem_limit_bytes=SMALL_VMEM),
        cost_estimate=cost(OVERLAP_FLOPS if weighted else 1e7, 4 * slots.total * slots.columns),
        name="combine_out" if weighted else "combine_in",
    )(ids, gains, back)


def fold_table(slots, shape, folded_dim):
    folded = iota(shape, folded_dim)
    plain = iota(shape, 1 - folded_dim)
    rem_bits = int(math.log2(slots.rem))
    exp_bits = int(math.log2(slots.exp_count))
    j = plain & (slots.rem - 1)
    source = (plain >> rem_bits) & (slots.exp_count - 1)
    f = plain >> (rem_bits + exp_bits)
    return (folded == source * slots.rows + f * slots.rem + j).astype(F32).astype(BF16)


def unpack_rows(slots, block):
    flat = block.reshape(slots.exp_count * slots.rows, slots.columns)
    if not slots.fold:
        return flat
    each = slots.exp_count * slots.rem
    plain = dot(
        fold_table(slots, (slots.blocks * each, slots.exp_count * slots.rows), 1),
        flat[:, slots.width :],
    ).astype(BF16)
    extra = jnp.concatenate(
        [plain[f * each : (f + 1) * each] for f in range(slots.blocks)], axis=1
    )
    return jnp.concatenate([flat[:, : slots.width], extra], axis=0)


def pack_rows(slots, rows, out_ref):
    count = slots.exp_count * slots.rows
    main = rows[:count].reshape(slots.exp_count, slots.rows, slots.width)
    out_ref[:, :, : slots.width] = main
    if slots.fold:
        each = slots.exp_count * slots.rem
        stacked = jnp.concatenate(
            [rows[count:, f * LANES : (f + 1) * LANES] for f in range(slots.blocks)], axis=0
        )
        folded = dot(fold_table(slots, (count, slots.blocks * each), 0), stacked).astype(BF16)
        out_ref[:, :, slots.width :] = folded.reshape(slots.exp_count, slots.rows, LANES)


def fetch(sources, targets, sems):
    copies = [
        pltpu.make_async_copy(source, target, sems.at[i])
        for i, (source, target) in enumerate(zip(sources, targets))
    ]
    for copy in copies:
        copy.start()
    return copies


def hold_kernel(expert_ref, gate_ref, up_ref, out_ref, sems):
    e = expert_ref[0]
    for copy in fetch([gate_ref.at[e], up_ref.at[e]], [out_ref.at[0], out_ref.at[1]], sems):
        copy.wait()


def hold(expert, gate_proj, up_proj):
    return expert_call(
        hold_kernel, "hold_weights", pltpu.VMEM((2, *gate_proj.shape[1:]), BF16), expert,
        in_hbm(gate_proj), in_hbm(up_proj), anywhere=(0, 1), copies=2,
    )


def expert_call(kernel, name, out_shape, scalars, *operands, anywhere=(), copies=0, held=None):
    in_vmem = pl.BlockSpec(memory_space=pltpu.VMEM)
    specs = [
        pl.BlockSpec(memory_space=pl.ANY) if i in anywhere else in_vmem
        for i in range(len(operands))
    ]
    if scalars is not None:
        specs = [pl.BlockSpec(memory_space=pltpu.SMEM)] + specs
        operands = (scalars, *operands)
    scratch = [] if held is None else [pltpu.VMEM(held, BF16)]
    if copies:
        scratch.append(pltpu.SemaphoreType.DMA((copies,)))
    return pl.pallas_call(
        kernel,
        in_specs=specs,
        out_specs=[in_vmem] * len(out_shape) if isinstance(out_shape, list) else in_vmem,
        out_shape=out_shape,
        scratch_shapes=scratch,
        compiler_params=pltpu.CompilerParams(vmem_limit_bytes=EXPERT_VMEM),
        name=name,
    )(*operands)


def gate_up_send_kernel(
    slots, order_ref, recv_ref, held_ref, gate_ref, up_ref, out_ref, next_ref, rows_ref, all_ref, sems
):
    e, following = order_ref[0], order_ref[1]
    copies = fetch(
        [recv_ref, gate_ref.at[following], up_ref.at[following]],
        [all_ref, next_ref.at[0], next_ref.at[1]],
        sems,
    )
    copies[0].wait()
    rows = unpack_rows(slots, all_ref[:, e])
    out_ref[0] = dot(rows, held_ref[0]).astype(BF16)
    out_ref[1] = dot(rows, held_ref[1]).astype(BF16)
    rows_ref[...] = unpack_rows(slots, all_ref[:, following])
    for copy in copies[1:]:
        copy.wait()


def gate_up_send(slots, order, recv, held, gate_proj, up_proj):
    out = [
        jax.ShapeDtypeStruct((2, slots.per_expert, gate_proj.shape[2]), BF16),
        pltpu.VMEM(held.shape, BF16),
        jax.ShapeDtypeStruct((slots.per_expert, slots.width), BF16),
    ]
    return expert_call(
        functools.partial(gate_up_send_kernel, slots), "gate_up_send", out, order,
        in_hbm(recv), held, in_hbm(gate_proj), in_hbm(up_proj),
        anywhere=(0, 2, 3), copies=3, held=recv.shape,
    )


def gate_up_keep_kernel(rows_ref, held_ref, arrived_ref, out_ref):
    for i in range(2):
        part = dot(rows_ref[...], held_ref[i]) + arrived_ref[i].astype(F32)
        out_ref[i] = part.astype(BF16)


def gate_up_keep(rows, held, arrived):
    out = jax.ShapeDtypeStruct(arrived.shape, BF16)
    return expert_call(gate_up_keep_kernel, "gate_up_keep", out, None, rows, held, arrived)


def hidden_grad_send_kernel(slots, order_ref, recv_ref, down_ref, out_ref, rows_ref):
    rows = unpack_rows(slots, recv_ref[:, order_ref[0]])
    out_ref[...] = dot(rows, down_ref[order_ref[0]], 1, 1).astype(BF16)
    rows_ref[...] = unpack_rows(slots, recv_ref[:, order_ref[1]])


def hidden_grad_send(slots, order, recv, down_proj):
    out = [
        jax.ShapeDtypeStruct((slots.per_expert, down_proj.shape[1]), BF16),
        jax.ShapeDtypeStruct((slots.per_expert, slots.width), BF16),
    ]
    kernel = functools.partial(hidden_grad_send_kernel, slots)
    return expert_call(kernel, "hidden_grad_send", out, order, recv, down_proj)


def hidden_grad_keep_kernel(expert_ref, rows_ref, down_ref, arrived_ref, out_ref):
    part = dot(rows_ref[...], down_ref[expert_ref[0]], 1, 1) + arrived_ref[...].astype(F32)
    out_ref[...] = part.astype(BF16)


def hidden_grad_keep(expert, rows, down_proj, arrived):
    out = jax.ShapeDtypeStruct(arrived.shape, BF16)
    return expert_call(
        hidden_grad_keep_kernel, "hidden_grad_keep", out, expert, rows, down_proj, arrived
    )


def store_rows(slots, rows, expert, packed_ref, out_ref, sem):
    pack_rows(slots, rows, packed_ref)
    copy = pltpu.make_async_copy(packed_ref, out_ref.at[:, expert], sem)
    copy.start()
    return copy


def packed_shape(slots):
    return (slots.exp_count, slots.local, slots.rows, slots.columns)


def packed_scratch(slots):
    return pltpu.VMEM((slots.local, slots.exp_count, slots.rows, slots.columns), BF16)


def route_out_kernel(slots, order_ref, mine_ref, other_ref, down_ref, out_ref, packed_ref, sems):
    stores = []
    for at, hidden_ref in enumerate((mine_ref, other_ref)):
        e = order_ref[at]
        rows = dot(hidden_ref[...], down_ref[e]).astype(BF16)
        stores.append(store_rows(slots, rows, e, packed_ref.at[at], out_ref, sems.at[at]))
    for store in stores:
        store.wait()


def route_out(slots, order, mine, other, down_proj):
    in_vmem = pl.BlockSpec(memory_space=pltpu.VMEM)
    return pl.pallas_call(
        functools.partial(route_out_kernel, slots),
        in_specs=[pl.BlockSpec(memory_space=pltpu.SMEM), in_vmem, in_vmem, in_vmem],
        out_specs=pl.BlockSpec(memory_space=pltpu.HBM),
        out_shape=pltpu.HBM(packed_shape(slots), BF16),
        scratch_shapes=[packed_scratch(slots), pltpu.SemaphoreType.DMA((slots.local,))],
        compiler_params=pltpu.CompilerParams(vmem_limit_bytes=EXPERT_VMEM),
        name="route_out",
    )(order, mine, other, down_proj)


def route_in_kernel(
    slots, order_ref, mine_ref, other_ref, held_ref, gate_ref, up_ref, out_ref,
    mine_held, other_held, next_ref, packed_ref, sems, out_sems,
):
    first, second = order_ref[0], order_ref[1]
    copies = fetch(
        [mine_ref, gate_ref.at[second], up_ref.at[second], other_ref],
        [mine_held, next_ref.at[0], next_ref.at[1], other_held],
        sems,
    )
    copies[0].wait()
    total = dot(mine_held[0], held_ref[0], 1, 1) + dot(mine_held[1], held_ref[1], 1, 1)
    rows = total.astype(BF16)
    stores = [store_rows(slots, rows, first, packed_ref.at[0], out_ref, out_sems.at[0])]
    for copy in copies[1:]:
        copy.wait()
    total = dot(other_held[0], next_ref[0], 1, 1) + dot(other_held[1], next_ref[1], 1, 1)
    rows = total.astype(BF16)
    stores.append(store_rows(slots, rows, second, packed_ref.at[1], out_ref, out_sems.at[1]))
    for store in stores:
        store.wait()


def route_in(slots, order, mine, other, held, gate_proj, up_proj):
    anywhere = pl.BlockSpec(memory_space=pl.ANY)
    return pl.pallas_call(
        functools.partial(route_in_kernel, slots),
        in_specs=[
            pl.BlockSpec(memory_space=pltpu.SMEM), anywhere, anywhere,
            pl.BlockSpec(memory_space=pltpu.VMEM), anywhere, anywhere,
        ],
        out_specs=pl.BlockSpec(memory_space=pltpu.HBM),
        out_shape=pltpu.HBM(packed_shape(slots), BF16),
        scratch_shapes=[
            pltpu.VMEM(mine.shape, BF16),
            pltpu.VMEM(other.shape, BF16),
            pltpu.VMEM(held.shape, BF16),
            packed_scratch(slots),
            pltpu.SemaphoreType.DMA((4,)),
            pltpu.SemaphoreType.DMA((slots.local,)),
        ],
        compiler_params=pltpu.CompilerParams(vmem_limit_bytes=EXPERT_VMEM),
        name="route_in",
    )(order, mine, other, held, in_hbm(gate_proj), in_hbm(up_proj))


def attention_kernel(offsets, tokens, chunk, first, last, me_ref, q_ref, g_ref, kv_ref, kv_far_ref, *refs):
    if not first:
        carry_ref, refs = refs[0], refs[3:]
    out_ref, qgrad_ref = refs[:2]
    if last:
        keep_ref, send_ref = refs[2:4]
    else:
        carried_ref = refs[2]
    scores_ref, low_ref, key_t, value_t, key_acc, value_acc = refs[-6:]
    d = HEAD_SIZE
    step = pl.program_id(0)
    me = me_ref[0]
    half = kv_ref.shape[0]
    seq = 2 * half
    scale = d ** (-0.5)
    to_base2 = scale * math.log2(math.e)

    @pl.when(step == 0)
    def _():
        for start, ref in ((0, kv_ref), (half, kv_far_ref)):
            for at in range(0, half, tokens):
                both = jnp.transpose(ref[at : at + tokens, :])
                key_t[:, start + at : start + at + tokens] = both[:d]
                value_t[:, start + at : start + at + tokens] = both[d:]
        if first:
            key_acc[...] = jnp.zeros_like(key_acc)
            value_acc[...] = jnp.zeros_like(value_acc)
        else:
            key_acc[...] = carry_ref[:, :d]
            value_acc[...] = carry_ref[:, d:]

    def piece(at, column):
        ref, start = (kv_ref, at) if at < half else (kv_far_ref, at - half)
        return ref[start : start + chunk, column : column + d]

    pairs = scores_ref.shape[0]
    lanes = scores_ref.shape[2]
    heads = lanes // tokens
    chunks = range(0, seq, chunk)
    ahead = iota((tokens, lanes), 0) - (iota((tokens, lanes), 1) & (tokens - 1))
    limits = [(me - (me ^ offset)) * tokens for offset in offsets]

    def columns(pair, h):
        start = (pair * heads + h) * d
        return slice(start, start + d)

    def stacked(ref, pair):
        return jnp.concatenate([ref[:, columns(pair, h)] for h in range(heads)], axis=0)

    every = range(pairs)
    q = [stacked(q_ref, pair) for pair in every]
    g = [stacked(g_ref, pair) for pair in every]
    g_t = [jnp.transpose(value) for value in g]
    top, inverse, row_dot = {}, {}, {}

    def keep_rows(ref, pair, value):
        low = value.astype(BF16)
        for h in range(heads):
            ref[:, columns(pair, h)] = jnp.transpose(low[:, h * tokens : (h + 1) * tokens])

    def score_stage(pair):
        largest = jnp.full((1, lanes), -jnp.inf, F32)
        for at in chunks:
            scores = dot(piece(at, 0), q[pair], 1, 1)
            for part in range(0, chunk, tokens):
                allowed = ahead <= limits[(at + part) // tokens]
                some = jnp.where(allowed, scores[part : part + tokens], -jnp.inf)
                scores_ref[pair, at + part : at + part + tokens, :] = some
                largest = jnp.maximum(largest, jnp.max(some, axis=0, keepdims=True))
            yield
        top[pair] = largest * to_base2

    def raise_stage(pair):
        total = jnp.zeros((1, lanes), F32)
        for at in chunks:
            raised = jnp.exp2(scores_ref[pair, at : at + chunk, :] * to_base2 - top[pair])
            scores_ref[pair, at : at + chunk, :] = raised
            total = total + jnp.sum(raised, axis=0, keepdims=True)
            yield
        inverse[pair] = 1.0 / total

    def attend_stage(pair):
        attended = jnp.zeros((d, lanes), F32)
        for at in chunks:
            low = (scores_ref[pair, at : at + chunk, :] * inverse[pair]).astype(BF16)
            low_ref[pair, at : at + chunk, :] = low
            attended = attended + dot(value_t[:, at : at + chunk], low)
            value_acc[at : at + chunk, :] += dot(low, g[pair])
            yield
        keep_rows(out_ref, pair, attended)
        attended = attended.astype(BF16).astype(F32)
        row_dot[pair] = jnp.sum(g_t[pair].astype(F32) * attended, axis=0, keepdims=True)

    def back_stage(pair):
        query_back = jnp.zeros((d, lanes), F32)
        for at in chunks:
            low = low_ref[pair, at : at + chunk, :]
            prob_grad = dot(piece(at, d), g_t[pair])
            score_grad = (low.astype(F32) * (prob_grad - row_dot[pair])).astype(BF16)
            query_back = query_back + dot(key_t[:, at : at + chunk], score_grad)
            key_acc[at : at + chunk, :] += dot(score_grad, q[pair])
            yield
        keep_rows(qgrad_ref, pair, query_back * scale)

    stages = (score_stage, raise_stage, attend_stage, back_stage)
    for slot in range(pairs + len(stages) - 1):
        running = [stages[slot - pair](pair) for pair in every if 0 <= slot - pair < len(stages)]
        while running:
            running = [stage for stage in running if next(stage, True) is None]

    @pl.when(step == pl.num_programs(0) - 1)
    def _():
        if last:
            keep_ref[:, :d] = (key_acc[:half, :] * scale).astype(BF16)
            keep_ref[:, d:] = value_acc[:half, :].astype(BF16)
            send_ref[:, :d] = (key_acc[half:, :] * scale).astype(BF16)
            send_ref[:, d:] = value_acc[half:, :].astype(BF16)
        else:
            carried_ref[:, :d] = key_acc[...]
            carried_ref[:, d:] = value_acc[...]


def attention(me, offsets, queries, attn_grad, kv_near, kv_far, part, parts, carried=None):
    tokens, columns = queries.shape
    half, both = kv_near.shape
    seq = 2 * half
    heads = columns // HEAD_SIZE
    group = 4 if heads % (4 * parts) == 0 and seq <= 2048 else 2 if heads % (2 * parts) == 0 else 1
    pairs = PAIRS if heads % (group * PAIRS * parts) == 0 and seq <= 2048 else 1
    lanes = group * tokens
    chunk = min(CHUNK, half)
    steps = heads // (group * pairs * parts)
    first, last = part == 0, part == parts - 1
    tile = pl.BlockSpec((tokens, pairs * group * HEAD_SIZE), lambda i, m: (0, i + part * steps))
    whole = pl.BlockSpec((half, both), lambda i, m: (0, 0))
    sums = pl.BlockSpec((seq, both), lambda i, m: (0, 0))
    held = pl.BlockSpec(memory_space=pl.ANY)
    wide = jax.ShapeDtypeStruct(queries.shape, BF16)
    if last:
        final = [jax.ShapeDtypeStruct((half, both), BF16)] * 2
    else:
        final = [jax.ShapeDtypeStruct((seq, both), F32)]
    return pl.pallas_call(
        functools.partial(attention_kernel, offsets, tokens, chunk, first, last),
        grid_spec=pltpu.PrefetchScalarGridSpec(
            num_scalar_prefetch=1,
            grid=(steps,),
            in_specs=[tile, tile, whole, whole] + ([] if first else [sums, held, held]),
            out_specs=[tile, tile] + ([whole, whole] if last else [sums]),
            scratch_shapes=[
                pltpu.VMEM((pairs, seq, lanes), F32),
                pltpu.VMEM((pairs, seq, lanes), BF16),
                pltpu.VMEM((HEAD_SIZE, seq), BF16),
                pltpu.VMEM((HEAD_SIZE, seq), BF16),
                pltpu.VMEM((seq, HEAD_SIZE), F32),
                pltpu.VMEM((seq, HEAD_SIZE), F32),
            ],
        ),
        out_shape=[wide, wide] + final,
        input_output_aliases={} if first else {6: 0, 7: 1},
        compiler_params=params(LARGE_VMEM),
        cost_estimate=cost(
            12 * tokens * columns * seq // parts,
            8 * tokens * columns // parts,
            tokens * heads * seq // parts,
        ),
        name="attention",
    )(me, in_hbm(queries), in_hbm(attn_grad), in_hbm(kv_near), kv_far, *(() if first else (carried[2], carried[0], carried[1])))


def swap(value, axis, bit):
    count = lax.axis_size(axis)
    return lax.ppermute(value, axis, [(i, i ^ bit) for i in range(count)])


def after(value, *earlier):
    return lax.optimization_barrier((value, *earlier))[0]


def far_bits(count):
    bits = []
    bit = count // 2
    while bit >= 1:
        bits.append(bit)
        bit //= 2
    return bits


def spread_sum(part, ctx_count, beside):
    result = None
    bit = 2
    while True:
        arrived = swap(part.astype(BF16), "ctx", bit)
        if result is None:
            result = beside(part)
            arrived = after(arrived, *result)
        bit *= 2
        if bit >= ctx_count:
            return (part, arrived), result
        part = part.astype(F32) + arrived.astype(F32)


def total_of(addends):
    return addends[0].astype(F32) + addends[1].astype(F32)


def activate(gate, up):
    return (jax.nn.silu(gate) * up).astype(BF16)


def gate_backward(hidden_grad, gate, up):
    s = jax.nn.sigmoid(gate)
    gate_back = (hidden_grad * up * s * (1.0 + gate * (1.0 - s))).astype(BF16)
    up_back = (hidden_grad * (gate * s)).astype(BF16)
    return jnp.stack([gate_back, up_back])


def body(
    queries, key_proj, value_matrix_rows, attn_grad, moe_input, moe_grad,
    expert_ids, route_weights, gate_proj, up_proj, down_proj,
):
    ctx_count = lax.axis_size("ctx")
    exp_count = lax.axis_size("exp")
    ctx_index = lax.axis_index("ctx")
    exp_index = lax.axis_index("exp")
    tokens = queries.shape[0]
    d = HEAD_SIZE
    kv_heads = key_proj.shape[1] // d
    sharers = ctx_count // kv_heads
    kv_head = ctx_index // sharers
    width = moe_input.shape[1]
    local = gate_proj.shape[0]
    expert_total = local * exp_count
    slot_count = 2 * ((tokens + expert_total - 2) // (expert_total - 1))
    slots = Slots(slot_count, width, exp_count, local)
    core = ctx_index % 2
    mine = core.astype(jnp.int32).reshape(1)
    other = 1 - mine
    order = jnp.concatenate([mine, other])
    shape = (exp_count, local, slots.rows, slots.columns)

    def exchange(rows):
        flat = rows.reshape(exp_count, local * slots.rows, slots.columns)
        return lax.all_to_all(flat, "exp", split_axis=0, concat_axis=0, tiled=True)

    me = exp_index.astype(jnp.int32).reshape(1)
    ids = expert_ids.T
    gains = route_weights.T

    kv = jnp.concatenate(
        [
            lax.dynamic_slice_in_dim(key_proj, kv_head * d, d, 1),
            lax.dynamic_slice_in_dim(value_matrix_rows, kv_head * d, d, 1),
        ],
        axis=1,
    )
    send_rows = dispatch(slots, False, ids, gains, moe_input)
    offsets = [0]
    kv_far = None
    for bit in far_bits(exp_count):
        if kv_far is not None:
            kv = jnp.concatenate([kv, after(kv_far, send_rows)], axis=0)
        if bit == 2:
            recv_rows = exchange(after(send_rows, kv)).reshape(shape)
        kv_far = swap(kv, "exp", bit)
        offsets = offsets + [o ^ bit for o in offsets]
    send_scaled = dispatch(slots, True, ids, gains, after(moe_grad, send_rows))
    held = hold(other, after(gate_proj, send_scaled), up_proj)

    def heads(part, carried, earlier):
        return attention(
            me, tuple(offsets), after(queries, earlier), attn_grad, kv, kv_far, part, 1, carried
        )

    recv_rows = after(recv_rows, kv)
    gu_send, held, rows = gate_up_send(slots, order[::-1], recv_rows, held, gate_proj, up_proj)
    gu_recv = swap(gu_send, "ctx", 1)
    gu_part = gate_up_keep(rows, held, gu_recv)
    recv_scaled = exchange(after(send_scaled, gu_part)).reshape(shape)
    gate_up_sum, (attn_out, query_grad, kv_keep, kv_send) = spread_sum(
        gu_part, ctx_count, lambda part: heads(0, None, part)
    )
    kv_recv = swap(kv_send, "exp", 1)
    hidden = activate(*total_of(gate_up_sum))
    hidden_other = swap(hidden, "ctx", 1)
    out_rows = route_out(slots, order, hidden, hidden_other, down_proj)
    back_out = exchange(out_rows).reshape(slots.total, slots.columns)

    hg_send, rows = hidden_grad_send(slots, order[::-1], after(recv_scaled, out_rows), down_proj)
    hg_recv = swap(hg_send, "ctx", 1)
    hg_part = hidden_grad_keep(mine, rows, down_proj, hg_recv)
    held = hold(mine, after(gate_proj, hg_part), up_proj)

    kv_sum = kv_keep.astype(F32) + after(kv_recv, hg_part).astype(F32)
    kv_low = kv_sum.astype(BF16)
    blocks = exp_count // 2
    kv_parts = [
        swap(kv_low[i * tokens : (i + 1) * tokens], "exp", offsets[i]) for i in range(1, blocks)
    ]
    gate_up_sum = [after(value, hg_part) for value in gate_up_sum]
    gate_up_total = total_of(gate_up_sum)
    hg_sum, _ = spread_sum(hg_part, ctx_count, lambda part: (kv_low, gate_up_total, held))
    back = gate_backward(total_of(hg_sum), *gate_up_total)
    back_other = swap(back, "ctx", 1)
    in_rows = route_in(slots, order, back, back_other, held, gate_proj, up_proj)
    kv_total = kv_sum[:tokens]
    for part in kv_parts:
        kv_total = kv_total + after(part, in_rows).astype(F32)
    kv_total = kv_total.astype(BF16)
    back_in = exchange(in_rows).reshape(slots.total, slots.columns)

    moe_out = combine(slots, True, ids, gains, after(back_out, kv_total))
    input_grad = combine(slots, False, ids, gains, back_in)

    kv_every = lax.all_gather(after(kv_total, in_rows), "ctx", axis=0, tiled=False)
    if sharers > 1:
        kv_every = kv_every.astype(F32).reshape(kv_heads, sharers, tokens, 2 * d).sum(axis=1)
    kv_every = kv_every.astype(BF16)
    key_grad = jnp.concatenate([kv_every[h, :, :d] for h in range(kv_heads)], axis=1)
    value_grad = jnp.concatenate([kv_every[h, :, d:] for h in range(kv_heads)], axis=1)
    return (attn_out, query_grad, key_grad, value_grad, moe_out, input_grad)


def solution(mesh):
    placed = (
        P("exp", "ctx"),
        P("exp", None),
        P("exp", None),
        P("exp", "ctx"),
        P("exp", "ctx"),
        P("exp", "ctx"),
        P("exp", None),
        P("exp", None),
        P("exp", "ctx", None),
        P("exp", "ctx", None),
        P("exp", None, "ctx"),
    )
    return jax.shard_map(
        body,
        mesh=mesh,
        in_specs=placed,
        out_specs=(
            P("exp", "ctx"),
            P("exp", "ctx"),
            P("exp", None),
            P("exp", None),
            P("exp", "ctx"),
            P("exp", "ctx"),
        ),
        check_vma=False,
    )
```
